512 devices in a mesh: dom: 32 (over y, x), ref: 16 (over z, core).
Axes of the slice: x: 4, y: 8, z: 8, core: 2. Of those that a mesh axis runs over, the one named last changes fastest.
Arguments:
- particles: bfloat16 [2, 4096, 8192], P(None, ('dom', 'ref')), may hold values from -512 to 512
- defocus: bfloat16 [4096], P(('dom', 'ref')), may hold values from 20 to 60
- references: bfloat16 [2, 512, 8192], P(None, 'ref'), may hold values from -5 to 5
- noise_weights: float32 [8192], replicated, may hold values from 0.005 to 0.05
Outputs:
- updated: float32 [2, 512, 8192], P(None, 'ref', 'dom')
The draws below stay inside these ranges and needn't reach their ends.
All inputs are finite; a program needn't handle non-finite values.
Results may differ from the reference program's by a relative error of at most 0.0065.
Values may be sent and summed in bfloat16 or wider, within the bound.
A program may use at most 64 MiB of HBM per device.

```python
import math
import jax
import jax.numpy as jnp
from jax import lax

EDGE = 128
PIX = 8192
TRANS = 4
NPART = 4096
NREF = 512


def shared_draw(key):
    ref_key = jax.random.fold_in(key, 11)
    focus_key = jax.random.fold_in(key, 12)
    ref_draw = jnp.clip(jax.random.normal(ref_key, (2, NREF, PIX), jnp.float32), -5.0, 5.0)
    focus_draw = jax.random.uniform(focus_key, (NPART,), jnp.float32, 20.0, 60.0)
    return (ref_draw, focus_draw)


def draw_contrast(focus_draw):
    half_edge = EDGE // 2
    pixel_index = jnp.arange(PIX, dtype=jnp.int32)
    freq_x = (pixel_index // half_edge - half_edge).astype(jnp.float32)
    freq_y = (pixel_index % half_edge).astype(jnp.float32)
    radius_sq = (freq_x * freq_x + freq_y * freq_y) / float(half_edge * half_edge)
    phases = focus_draw[:, None] * radius_sq[None, :]
    return -(0.995 * jnp.sin(phases) + 0.1 * jnp.cos(phases))


def draw_particles(key, part):
    ref_draw, focus_draw = shared_draw(key)
    key = jax.random.fold_in(key, 3)
    key_noise = jax.random.fold_in(key, 0)
    key_pick = jax.random.fold_in(key, 2)
    key_amplitude = jax.random.fold_in(key, 3)
    chosen = jax.random.randint(key_pick, (NPART,), 0, NREF)
    amplitude = jax.random.uniform(key_amplitude, (NPART,), jnp.float32, 3.0, 6.0)
    aligned = jnp.arange(NPART) % 16 == 0
    signal = ref_draw[:, chosen, :] * (amplitude[:, None] * draw_contrast(focus_draw))[None]
    noise_part = jnp.clip(jax.random.normal(key_noise, (2, NPART, PIX), jnp.float32), -6.0, 6.0)
    drawn = jnp.clip(noise_part + jnp.where(aligned[None, :, None], signal, 0.0), -512.0, 512.0)
    return drawn.astype(jnp.bfloat16)


def draw_defocus(key, part):
    ref_draw, focus_draw = shared_draw(key)
    return focus_draw.astype(jnp.bfloat16)


def draw_references(key, part):
    ref_draw, focus_draw = shared_draw(key)
    return ref_draw.astype(jnp.bfloat16)


def setup_inputs(seed: int = 0) -> dict:
    key_of = jax.random.split(jax.random.key(seed), 5)
    particles = draw_particles(jax.random.fold_in(key_of[4], 71), 0)
    defocus = draw_defocus(jax.random.fold_in(key_of[4], 71), 0)
    references = draw_references(jax.random.fold_in(key_of[4], 71), 0)
    noise_weights = jnp.clip(jnp.exp(jax.random.uniform(key_of[3], (PIX,), jnp.float32, math.log(0.005), math.log(0.05))), 0.005, 0.05)
    return {"particles": particles, "defocus": defocus, "references": references, "noise_weights": noise_weights}


CONTRAST_SIN = 0.995
CONTRAST_COS = 0.1
SHIFT_PIXELS = 2.0
REGULARIZER = 0.05


def frequencies():
    half_edge = EDGE // 2
    pixel_index = jnp.arange(PIX, dtype=jnp.int32)
    freq_x = (pixel_index // half_edge - half_edge).astype(jnp.float32)
    freq_y = (pixel_index % half_edge).astype(jnp.float32)
    return freq_x, freq_y


def contrast(focus, freq_x, freq_y):
    half_edge = EDGE // 2
    radius_sq = (freq_x * freq_x + freq_y * freq_y) / float(half_edge * half_edge)
    phases = focus.astype(jnp.float32)[:, None] * radius_sq[None, :]
    return -(CONTRAST_SIN * jnp.sin(phases) + CONTRAST_COS * jnp.cos(phases))


def weighting(images, focus, noise_weights, freq_x, freq_y):
    transfer = contrast(focus, freq_x, freq_y)
    factor = noise_weights[None, :] * transfer
    weighted = (images.astype(jnp.float32) * factor[None]).astype(jnp.bfloat16)
    ctf_weight = (factor * transfer).astype(jnp.bfloat16)
    return weighted, ctf_weight


def shift_tables(freq_x, freq_y):
    shift_ids = jnp.arange(TRANS, dtype=jnp.int32)
    move_x = SHIFT_PIXELS * (shift_ids % 2).astype(jnp.float32)
    move_y = SHIFT_PIXELS * (shift_ids // 2).astype(jnp.float32)
    angles = 2.0 * math.pi * (move_x[:, None] * freq_x[None, :] + move_y[:, None] * freq_y[None, :]) / float(EDGE)
    return jnp.cos(angles), jnp.sin(angles)


def shifted_references(references, cos_table, sin_table):
    ref_real = references[0].astype(jnp.float32)
    ref_imag = references[1].astype(jnp.float32)
    real_part = ref_real[None] * cos_table[:, None, :] - ref_imag[None] * sin_table[:, None, :]
    imag_part = ref_real[None] * sin_table[:, None, :] + ref_imag[None] * cos_table[:, None, :]
    ref_count = references.shape[1]
    shifted = jnp.stack([real_part, imag_part]).reshape(2, TRANS * ref_count, -1).astype(jnp.bfloat16)
    power = (ref_real * ref_real + ref_imag * ref_imag).astype(jnp.bfloat16)
    return shifted, power


def reference(particles, defocus, references, noise_weights):
    freq_x, freq_y = frequencies()
    cos_table, sin_table = shift_tables(freq_x, freq_y)
    shifted, power = shifted_references(references, cos_table, sin_table)
    weighted, ctf_weight = weighting(particles, defocus, noise_weights, freq_x, freq_y)
    weighted_wide = lax.optimization_barrier(weighted).astype(jnp.float32)
    shifted_wide = lax.optimization_barrier(shifted).astype(jnp.float32)
    cross_term = jnp.einsum("cnp,cmp->nm", weighted_wide, shifted_wide)
    ctf_term = jnp.dot(ctf_weight, power.T, preferred_element_type=jnp.float32)
    scores = cross_term - 0.5 * jnp.tile(ctf_term, (1, TRANS))
    row_top = jnp.max(scores, axis=1, keepdims=True)
    row_sum = jnp.sum(jnp.exp(scores - row_top), axis=1, keepdims=True)
    log_norm = row_top + jnp.log(row_sum)
    posterior = jnp.exp(scores - log_norm).astype(jnp.bfloat16)
    posterior_wide = lax.optimization_barrier(posterior).astype(jnp.float32)
    occupancy = jnp.sum(posterior_wide.reshape(NPART, TRANS, NREF), axis=1).astype(jnp.bfloat16)
    real_sum = jnp.zeros((NREF, PIX), jnp.float32)
    imag_sum = jnp.zeros((NREF, PIX), jnp.float32)
    for shift_index in range(TRANS):
        columns = posterior_wide[:, shift_index * NREF:(shift_index + 1) * NREF]
        per_shift = jnp.einsum("nm,cnp->cmp", columns, weighted_wide)
        real_sum = real_sum + per_shift[0] * cos_table[shift_index] + per_shift[1] * sin_table[shift_index]
        imag_sum = imag_sum + per_shift[1] * cos_table[shift_index] - per_shift[0] * sin_table[shift_index]
    ctf_sums = jnp.dot(occupancy.T, ctf_weight, preferred_element_type=jnp.float32)
    return jnp.stack([real_sum, imag_sum]) / (ctf_sums[None] + REGULARIZER)
```

```python
import jax
import jax.numpy as jnp
from jax import lax
from jax.experimental import pallas as pl
from jax.experimental.pallas import tpu as pltpu
from jax.sharding import PartitionSpec as P

PIX = 8192
TRANS = 4
REFS = 32
SX, SY, SZ = 4, 8, 8
NCHUNK = 4
CHUNK = PIX // NCHUNK
SLICE = 1024
OUT = 256
REGULARIZER = 0.05

AMP = 1.000012499921876
PHASE = 0.015941940272471127
INV_TWO_PI = 0.15915494309189535
SIN_TERMS = (
    6.283182818554191,
    -41.341421398928475,
    81.5961838781331,
    -76.58010057017961,
    41.205395033387106,
    -12.271262585212861,
)

MESH = pl.DeviceIdType.MESH
F32 = jnp.float32
BF16 = jnp.bfloat16


def sin_turns(turns):
    v = turns - jnp.round(turns)
    sq = v * v
    acc = sq * SIN_TERMS[5] + SIN_TERMS[4]
    for term in SIN_TERMS[3::-1]:
        acc = acc * sq + term
    return acc * v


def nt_dot(a, b):
    return lax.dot_general(a, b, (((1,), (1,)), ((), ())), preferred_element_type=F32)


def twice(a):
    return jnp.concatenate([a, a], axis=0)


def kernel(
    part_ref, focus_ref, refs_ref, noise_ref, out_ref,
    gath, focus, tab, factor, wgt, cwt, shf, pwr, score, cterm, stat, post, occ,
    xsend, xrecv, ysend, yrecv, own_sum,
    local_sem, ring_send, ring_recv, core_send, core_recv,
    fsend, frecv, ssend, srecv, xs_sem, xr_sem, ys_sem, yr_sem,
):
    dom, me = lax.axis_index("dom"), lax.axis_index("ref")
    y, x, z, c = dom // SX, dom % SX, me // 2, me % 2
    other = (dom, z * 2 + 1 - c)
    up = (dom, lax.rem(z + 1, SZ) * 2 + c)
    down = (dom, lax.rem(z + SZ - 1, SZ) * 2 + c)

    def mate(step):
        return lax.rem(me + step, 2 * SZ)

    def x_mate(step):
        return (y * SX + lax.rem(x + step, SX), me)

    def y_mate(step):
        return (lax.rem(y + step, SY) * SX + x, me)

    barrier = pltpu.get_barrier_semaphore()
    for step in range(1, 2 * SZ):
        pl.semaphore_signal(barrier, inc=1, device_id=(dom, mate(step)), device_id_type=MESH)
    for step in range(1, SX):
        pl.semaphore_signal(barrier, inc=1, device_id=x_mate(step), device_id_type=MESH)
    for step in range(1, SY):
        pl.semaphore_signal(barrier, inc=1, device_id=y_mate(step), device_id_type=MESH)
    own = pltpu.make_async_copy(part_ref, gath.at[me], local_sem)
    own.start()
    focus[me] = focus_ref[...]
    own.wait()
    pl.semaphore_wait(barrier, 2 * SZ - 1 + SX - 1 + SY - 1)

    def cols(j):
        return pl.ds(pl.multiple_of(j * CHUNK, CHUNK), CHUNK)

    def ring_copy(way, step, j):
        block = lax.rem(z + SZ - step, SZ) if way == 0 else lax.rem(z + step, SZ)
        ref = gath.at[block * 2 + c, :, cols(j)]
        return pltpu.make_async_remote_copy(
            ref, ref, ring_send.at[way, step, j], ring_recv.at[way, step, j],
            device_id=up if way == 0 else down, device_id_type=MESH,
        )

    def ring_landed(way, step, j):
        block = lax.rem(z + 2 * SZ - step - 1, SZ) if way == 0 else lax.rem(z + step + 1, SZ)
        ref = gath.at[block * 2 + c, :, cols(j)]
        pltpu.make_async_remote_copy(
            ref, ref, ring_send.at[way, step, j], ring_recv.at[way, step, j],
            device_id=up if way == 0 else down, device_id_type=MESH,
        ).wait_recv()

    def core_copy(dist, j):
        ref = gath.at[lax.rem(z + dist, SZ) * 2 + c, :, cols(j)]
        return pltpu.make_async_remote_copy(
            ref, ref, core_send.at[dist, j], core_recv.at[dist, j],
            device_id=other, device_id_type=MESH,
        )

    def core_landed(dist, j):
        ref = gath.at[lax.rem(z + dist, SZ) * 2 + 1 - c, :, cols(j)]
        pltpu.make_async_remote_copy(
            ref, ref, core_send.at[dist, j], core_recv.at[dist, j],
            device_id=other, device_id_type=MESH,
        ).wait_recv()

    def focus_copy(step):
        return pltpu.make_async_remote_copy(
            focus.at[me], focus.at[me], fsend.at[step - 1], frecv.at[step - 1],
            device_id=(dom, mate(step)), device_id_type=MESH,
        )

    def focus_landed(step):
        ref = focus.at[lax.rem(me + 2 * SZ - step, 2 * SZ)]
        pltpu.make_async_remote_copy(
            ref, ref, fsend.at[step - 1], frecv.at[step - 1],
            device_id=(dom, mate(step)), device_id_type=MESH,
        ).wait_recv()

    def stat_copy(step):
        return pltpu.make_async_remote_copy(
            stat.at[me], stat.at[me], ssend.at[step - 1], srecv.at[step - 1],
            device_id=(dom, mate(step)), device_id_type=MESH,
        )

    def stat_landed(step):
        ref = stat.at[lax.rem(me + 2 * SZ - step, 2 * SZ)]
        pltpu.make_async_remote_copy(
            ref, ref, ssend.at[step - 1], srecv.at[step - 1],
            device_id=(dom, mate(step)), device_id_type=MESH,
        ).wait_recv()

    for j in range(NCHUNK):
        ring_copy(0, 0, j).start()
        ring_copy(1, 0, j).start()
    for step in range(1, 2 * SZ):
        focus_copy(step).start()
    for j in range(NCHUNK):
        core_copy(0, j).start()

    def tables_and_shifts(k):
        at = pl.ds(pl.multiple_of(k * SLICE, SLICE), SLICE)
        pixel = lax.broadcasted_iota(jnp.int32, (8, SLICE), 1) + k * SLICE
        fx = (lax.shift_right_logical(pixel, 6) - 64).astype(F32)
        fy = (pixel & 63).astype(F32)
        tab[0, :, at] = (fx * fx + fy * fy) * (INV_TWO_PI / 4096.0)
        trig = []
        for turns in (fx * (1.0 / 64.0), fy * (1.0 / 64.0), (fx + fy) * (1.0 / 64.0)):
            cos, sin = sin_turns(turns + 0.25), sin_turns(turns)
            trig.append((cos, sin))
        for t, (cos, sin) in enumerate(trig):
            tab[1 + 2 * t, :, at] = cos
            tab[2 + 2 * t, :, at] = sin
        for half in range(REFS // 16):
            rows = slice(16 * half, 16 * half + 16)
            real, imag = refs_ref[0, rows, at], refs_ref[1, rows, at]
            shf[0, rows, at] = real
            shf[1, rows, at] = imag
            real, imag = real.astype(F32), imag.astype(F32)
            power = (real * real + imag * imag).astype(BF16)
            for t in range(TRANS):
                to = slice(t * REFS + 16 * half, t * REFS + 16 * half + 16)
                pwr[to, at] = power
                if t:
                    cos, sin = twice(trig[t - 1][0]), twice(trig[t - 1][1])
                    shf[0, to, at] = (real * cos - imag * sin).astype(BF16)
                    shf[1, to, at] = (real * sin + imag * cos).astype(BF16)

    def contrast(k):
        at = pl.ds(pl.multiple_of(k * SLICE, SLICE), SLICE)

        def rows16(i, _):
            rows = pl.ds(pl.multiple_of(i * 16, 16), 16)
            turns = twice(tab[0, :, at])
            d0, d1 = focus[2 * i], focus[2 * i + 1]
            d = jnp.concatenate([d0, d1], axis=0)[:, :1]
            transfer = sin_turns(turns * d + PHASE) * (-AMP)
            fac = transfer * noise_ref[:, at]
            factor[rows, at] = fac
            cwt[rows, at] = (fac * transfer).astype(BF16)
            return 0

        lax.fori_loop(0, SZ, rows16, 0)
        cterm[...] += nt_dot(pwr[:, at], cwt[:, at])

    def events(e, j_all):
        del j_all
        step, j = e // NCHUNK, lax.rem(e, NCHUNK)
        for s in range(SZ // 2):

            @pl.when(step == s)
            def _():
                if s < 3:
                    for way in range(2):
                        ring_landed(way, s, j)
                    if s < 2:
                        for way in range(2):
                            ring_copy(way, s + 1, j).start()
                    else:

                        @pl.when(j < 2)
                        def _():
                            ring_copy(0, 3, j).start()

                        @pl.when(j >= 2)
                        def _():
                            ring_copy(1, 3, j).start()

                    core_copy(SZ - 1 - s, j).start()
                    core_copy(s + 1, j).start()
                else:

                    @pl.when(j < 2)
                    def _():
                        ring_landed(0, 3, j)

                    @pl.when(j >= 2)
                    def _():
                        ring_landed(1, 3, j)

                    core_copy(4, j).start()

    cterm[...] = jnp.zeros_like(cterm)

    def first(e, _):
        tables_and_shifts(e)
        events(e, None)
        return 0

    lax.fori_loop(0, 8, first, 0)
    for step in range(1, 2 * SZ):
        focus_landed(step)

    def second(e, _):
        contrast(2 * e)
        contrast(2 * e + 1)
        events(e + 8, None)
        return 0

    lax.fori_loop(0, 4, second, 0)

    score[...] = jnp.zeros_like(score)

    def third(j, _):
        events(j + 12, None)
        at = cols(j)
        for dist in range(SZ):
            core_landed(dist, j)

        def weigh(i, _):
            rows = pl.ds(pl.multiple_of(i * 16, 16), 16)
            fac = factor[rows, at]
            a = gath[2 * i, :, at].astype(F32)
            b = gath[2 * i + 1, :, at].astype(F32)
            for comp in range(2):
                pick = slice(8 * comp, 8 * comp + 8)
                wgt[comp, rows, at] = (
                    jnp.concatenate([a[pick], b[pick]], axis=0) * fac
                ).astype(BF16)
            return 0

        lax.fori_loop(0, SZ, weigh, 0)
        score[...] += nt_dot(shf[0, :, at], wgt[0, :, at]) + nt_dot(shf[1, :, at], wgt[1, :, at])
        return 0

    lax.fori_loop(0, NCHUNK, third, 0)

    scores = score[...] - 0.5 * cterm[...]
    top = jnp.max(scores, axis=0, keepdims=True)
    total = jnp.sum(jnp.exp(scores - top), axis=0, keepdims=True)
    stat[me] = jnp.concatenate([top, total, jnp.zeros((6, 128), F32)], axis=0)
    for step in range(1, 2 * SZ):
        stat_copy(step).start()
    score[...] = scores
    for step in range(1, 2 * SZ):
        stat_landed(step)
    stats = stat[...]
    tops, totals = stats[:, 0, :], stats[:, 1, :]
    all_top = jnp.max(tops, axis=0, keepdims=True)
    all_total = jnp.sum(totals * jnp.exp(tops - all_top), axis=0, keepdims=True)
    log_norm = all_top + jnp.log(all_total)
    posterior = jnp.exp(score[...] - log_norm).astype(BF16)
    post[...] = posterior
    wide = posterior.astype(F32)
    occ[...] = (
        wide[0:REFS] + wide[REFS : 2 * REFS] + wide[2 * REFS : 3 * REFS] + wide[3 * REFS :]
    ).astype(BF16)

    def y_step(i):
        return 4 + (1 - 2 * lax.rem(i, 2)) * ((i + 1) // 2)

    def x_copy(i, step):
        return pltpu.make_async_remote_copy(
            xsend.at[i, lax.rem(x + step, SX)], xrecv.at[i, step - 1],
            xs_sem.at[i, step - 1], xr_sem.at[i, step - 1],
            device_id=x_mate(step), device_id_type=MESH,
        )

    def y_copy(i):
        step = y_step(i)
        return pltpu.make_async_remote_copy(
            ysend.at[i], yrecv.at[i], ys_sem.at[i], yr_sem.at[i],
            device_id=y_mate(step), device_id_type=MESH,
        )

    def piece(i, _):
        base = lax.rem(y + y_step(i), SY) * SLICE

        def quarter(q, _):
            at = pl.ds(pl.multiple_of(base + q * OUT, OUT), OUT)
            a0 = jnp.dot(post[...], wgt[0, :, at], preferred_element_type=F32)
            a1 = jnp.dot(post[...], wgt[1, :, at], preferred_element_type=F32)
            ctf = jnp.dot(occ[...], cwt[:, at], preferred_element_type=F32)
            real, imag = a0[0:REFS], a1[0:REFS]
            for t in range(1, TRANS):
                cos, sin = tab[2 * t - 1, :, at], tab[2 * t, :, at]
                cos = jnp.concatenate([cos] * (REFS // 8), axis=0)
                sin = jnp.concatenate([sin] * (REFS // 8), axis=0)
                b0, b1 = a0[t * REFS : (t + 1) * REFS], a1[t * REFS : (t + 1) * REFS]
                real = real + b0 * cos + b1 * sin
                imag = imag + b1 * cos - b0 * sin
            xsend[i, q, 0:REFS] = real.astype(BF16)
            xsend[i, q, REFS : 2 * REFS] = imag.astype(BF16)
            xsend[i, q, 2 * REFS :] = ctf.astype(BF16)
            return 0

        lax.fori_loop(0, SX, quarter, 0)
        for step in range(1, SX):
            x_copy(i, step).start()
        return 0

    lax.fori_loop(0, SY, piece, 0)

    def x_total(i):
        for step in range(1, SX):
            x_copy(i, step).wait_recv()
        acc = xsend[i, x].astype(F32)
        for step in range(1, SX):
            acc = acc + xrecv[i, step - 1].astype(F32)
        return acc

    def forward(i, _):
        ysend[i] = x_total(i).astype(BF16)
        y_copy(i).start()
        return 0

    lax.fori_loop(0, SY - 1, forward, 0)
    own_sum[...] = x_total(SY - 1)

    def collect(i, _):
        y_copy(i).wait_recv()
        own_sum[...] += yrecv[i].astype(F32)
        return 0

    lax.fori_loop(0, SY - 1, collect, 0)
    weight = own_sum[2 * REFS :] + REGULARIZER
    out_ref[0] = own_sum[0:REFS] / weight
    out_ref[1] = own_sum[REFS : 2 * REFS] / weight

    def drain_ring(e, _):
        j = lax.rem(e, NCHUNK)
        for s in range(SZ // 2):

            @pl.when(e // NCHUNK == s)
            def _():
                if s < 3:
                    ring_copy(0, s, j).wait_send()
                    ring_copy(1, s, j).wait_send()
                else:

                    @pl.when(j < 2)
                    def _():
                        ring_copy(0, 3, j).wait_send()

                    @pl.when(j >= 2)
                    def _():
                        ring_copy(1, 3, j).wait_send()

        return 0

    lax.fori_loop(0, 16, drain_ring, 0)

    def drain_core(dist, _):
        for j in range(NCHUNK):
            core_copy(dist, j).wait_send()
        return 0

    lax.fori_loop(0, SZ, drain_core, 0)

    def drain_mates(step, _):
        focus_copy(step).wait_send()
        stat_copy(step).wait_send()
        return 0

    lax.fori_loop(1, 2 * SZ, drain_mates, 0)

    def drain_sums(i, _):
        for step in range(1, SX):
            x_copy(i, step).wait_send()
        return 0

    lax.fori_loop(0, SY, drain_sums, 0)

    def drain_y(i, _):
        y_copy(i).wait_send()
        return 0

    lax.fori_loop(0, SY - 1, drain_y, 0)


def shards(particles, defocus, references, noise_weights):
    dma = pltpu.SemaphoreType.DMA
    nref = TRANS * REFS
    nblock = 2 * SZ
    rows = particles.shape[0] * particles.shape[1]
    focus = jnp.broadcast_to(defocus.astype(F32)[:, None], (8, 128))
    vmem = pl.BlockSpec(memory_space=pltpu.VMEM)
    return pl.pallas_call(
        kernel,
        out_shape=jax.ShapeDtypeStruct((2, REFS, OUT), F32),
        in_specs=[pl.BlockSpec(memory_space=pl.ANY), vmem, vmem, vmem],
        out_specs=vmem,
        scratch_shapes=[
            pltpu.VMEM((nblock, rows, PIX), BF16),
            pltpu.VMEM((nblock, 8, 128), F32),
            pltpu.VMEM((7, 8, PIX), F32),
            pltpu.VMEM((128, PIX), F32),
            pltpu.VMEM((2, 128, PIX), BF16),
            pltpu.VMEM((128, PIX), BF16),
            pltpu.VMEM((2, nref, PIX), BF16),
            pltpu.VMEM((nref, PIX), BF16),
            pltpu.VMEM((nref, 128), F32),
            pltpu.VMEM((nref, 128), F32),
            pltpu.VMEM((nblock, 8, 128), F32),
            pltpu.VMEM((nref, 128), BF16),
            pltpu.VMEM((REFS, 128), BF16),
            pltpu.VMEM((SY, SX, 3 * REFS, OUT), BF16),
            pltpu.VMEM((SY, SX - 1, 3 * REFS, OUT), BF16),
            pltpu.VMEM((SY - 1, 3 * REFS, OUT), BF16),
            pltpu.VMEM((SY - 1, 3 * REFS, OUT), BF16),
            pltpu.VMEM((3 * REFS, OUT), F32),
            dma,
            dma((2, 4, NCHUNK)),
            dma((2, 4, NCHUNK)),
            dma((SZ, NCHUNK)),
            dma((SZ, NCHUNK)),
            dma((nblock - 1,)),
            dma((nblock - 1,)),
            dma((nblock - 1,)),
            dma((nblock - 1,)),
            dma((SY, SX - 1)),
            dma((SY, SX - 1)),
            dma((SY - 1,)),
            dma((SY - 1,)),
        ],
        name="expectation",
        compiler_params=pltpu.CompilerParams(
            collective_id=0, has_side_effects=True, vmem_limit_bytes=56 * 2**20
        ),
    )(particles.reshape(rows, PIX), focus, references, noise_weights.reshape(1, PIX))


def solution(mesh):
    return jax.shard_map(
        shards,
        mesh=mesh,
        in_specs=(P(None, ("dom", "ref"), None), P(("dom", "ref")), P(None, "ref", None), P()),
        out_specs=P(None, "ref", "dom"),
        check_vma=False,
    )
```

```python
import jax
import jax.numpy as jnp
from jax import lax
from jax.experimental import pallas as pl
from jax.experimental.pallas import tpu as pltpu
from jax.sharding import PartitionSpec as P

PIX = 8192
TRANS = 4
REFS = 32
SX, SY, SZ = 4, 8, 8
OUT = 256
ROW = SX * OUT
LOCAL = SY * OUT
WIDE = LOCAL + 128
PART = 512
HALF = SX // 2
NREF = TRANS * REFS
NPART = SZ * SX * 16
REGULARIZER = 0.05

AMP = 1.000012499921876
PHASE = 0.015941940272471127
INV_TWO_PI = 0.15915494309189535
SIN_TERMS = (
    6.283182818554191,
    -41.341421398928475,
    81.5961838781331,
    -76.58010057017961,
    41.205395033387106,
    -12.271262585212861,
)

MESH = pl.DeviceIdType.MESH
F32 = jnp.float32
BF16 = jnp.bfloat16


def sin_turns(turns):
    v = turns - jnp.round(turns)
    sq = v * v
    acc = sq * SIN_TERMS[5] + SIN_TERMS[4]
    for term in SIN_TERMS[3::-1]:
        acc = acc * sq + term
    return acc * v


def nt_dot(a, b):
    return lax.dot_general(a, b, (((1,), (1,)), ((), ())), preferred_element_type=F32)


def twice(a):
    return jnp.concatenate([a, a], axis=0)


def kernel(
    part_ref, focus_ref, refs_ref, noise_ref, out_ref,
    gath, focus, refs, tab, wgt, shf, score, stat, flip, post, occ, ysend, yrecv, total,
    local_sem, refs_sem, asend, arecv, ring_send, ring_recv, core_send, core_recv,
    tsend, trecv, ssend, srecv, ys_sem, yr_sem,
):
    dom, me = lax.axis_index("dom"), lax.axis_index("ref")
    y, x, z, c = dom // SX, dom % SX, me // 2, me % 2
    other = (dom, z * 2 + 1 - c)
    up = (dom, lax.rem(z + 1, SZ) * 2 + c)
    down = (dom, lax.rem(z + SZ - 1, SZ) * 2 + c)

    def remote(src, dst, send, recv, device):
        return pltpu.make_async_remote_copy(
            src, dst, send, recv, device_id=device, device_id_type=MESH
        )

    def mate(step):
        return (dom, lax.rem(me + step, 2 * SZ))

    def x_mate(step):
        return (y * SX + lax.rem(x + step, SX), me)

    def y_mate(step):
        return (lax.rem(y + step, SY) * SX + x, me)

    def source(o):
        return lax.rem(x + SX - o, SX)

    def strip(q, to):
        return pl.ds(pl.multiple_of(q * ROW + to * OUT, OUT), OUT)

    def local(q):
        return pl.ds(pl.multiple_of(q * OUT, OUT), OUT)

    barrier = pltpu.get_barrier_semaphore()
    for step in range(1, 2 * SZ):
        pl.semaphore_signal(barrier, inc=1, device_id=mate(step), device_id_type=MESH)
    for step in range(1, SX):
        pl.semaphore_signal(barrier, inc=1, device_id=x_mate(step), device_id_type=MESH)
    for step in range(1, SY):
        pl.semaphore_signal(barrier, inc=1, device_id=y_mate(step), device_id_type=MESH)

    for q in range(SY):
        pltpu.make_async_copy(
            part_ref.at[:, strip(q, x)], gath.at[me, x, :, local(q)], local_sem
        ).start()
    for q in range(SY):
        pltpu.make_async_copy(
            refs_ref.at[:, :, strip(q, x)], refs.at[:, :, local(q)], refs_sem
        ).start()
    diagonal = lax.broadcasted_iota(jnp.int32, (8, 8), 0) == lax.broadcasted_iota(
        jnp.int32, (8, 8), 1
    )
    wide = jnp.broadcast_to(focus_ref[...].astype(F32), (8, 8))
    column = jnp.sum(jnp.where(diagonal, wide, 0.0), axis=1, keepdims=True)
    spread = twice(jnp.broadcast_to(column, (8, 128))).astype(BF16)
    focus[...] = spread
    gath[me, x, :, LOCAL:] = spread
    here = gath.at[me, x, :, pl.ds(0, LOCAL)]
    pltpu.make_async_copy(here, here, local_sem).wait()
    pl.semaphore_wait(barrier, 2 * SZ - 1 + SX - 1 + SY - 1)

    def ring_copy(way, step, o):
        block = lax.rem(z + SZ - step, SZ) if way == 0 else lax.rem(z + step, SZ)
        ref = gath.at[block * 2 + c, source(o)]
        return remote(
            ref, ref, ring_send.at[way, step, o], ring_recv.at[way, step, o],
            up if way == 0 else down,
        )

    def ring_landed(way, step, o):
        block = lax.rem(z + 2 * SZ - step - 1, SZ) if way == 0 else lax.rem(z + step + 1, SZ)
        ref = gath.at[block * 2 + c, source(o)]
        remote(
            ref, ref, ring_send.at[way, step, o], ring_recv.at[way, step, o],
            up if way == 0 else down,
        ).wait_recv()

    def core_copy(dist, o):
        ref = gath.at[lax.rem(z + dist, SZ) * 2 + c, source(o)]
        return remote(ref, ref, core_send.at[dist, o], core_recv.at[dist, o], other)

    def core_landed(dist, o):
        ref = gath.at[lax.rem(z + dist, SZ) * 2 + 1 - c, source(o)]
        remote(ref, ref, core_send.at[dist, o], core_recv.at[dist, o], other).wait_recv()

    def swap_landed(o):
        ref = gath.at[me, source(o)]
        remote(ref, ref, asend.at[o - 1], arecv.at[o - 1], x_mate(o)).wait_recv()

    def term_copy(dist, o):
        ref = score.at[x, lax.rem(z + dist, SZ)]
        return remote(ref, ref, tsend.at[dist, o - 1], trecv.at[dist, o - 1], x_mate(o))

    def term_landed(dist, o):
        ref = score.at[source(o), lax.rem(z + dist, SZ)]
        remote(ref, ref, tsend.at[dist, o - 1], trecv.at[dist, o - 1], x_mate(o)).wait_recv()

    def stat_copy(step):
        return remote(
            stat.at[me], stat.at[me], ssend.at[step - 1], srecv.at[step - 1], mate(step)
        )

    def stat_landed(step):
        ref = stat.at[lax.rem(me + 2 * SZ - step, 2 * SZ)]
        remote(ref, ref, ssend.at[step - 1], srecv.at[step - 1], mate(step)).wait_recv()

    ring_copy(0, 0, 0).start()
    ring_copy(1, 0, 0).start()
    for o in range(1, SX):
        to = lax.rem(x + o, SX)
        for q in range(SY):
            remote(
                part_ref.at[:, strip(q, to)], gath.at[me, x, :, local(q)],
                asend.at[o - 1], arecv.at[o - 1], x_mate(o),
            ).start()
        remote(
            focus, gath.at[me, x, :, pl.ds(LOCAL, 128)],
            asend.at[o - 1], arecv.at[o - 1], x_mate(o),
        ).start()
    core_copy(0, 0).start()
    pltpu.make_async_copy(refs, refs, refs_sem).wait()

    def tables_and_shifts(q, _):
        at = local(q)
        pixel = lax.broadcasted_iota(jnp.int32, (8, OUT), 1) + (q * ROW + x * OUT)
        fx = (lax.shift_right_logical(pixel, 6) - 64).astype(F32)
        fy = (pixel & 63).astype(F32)
        tab[0, :, at] = (fx * fx + fy * fy) * (INV_TWO_PI / 4096.0)
        tab[7, :, at] = jnp.broadcast_to(noise_ref[:, strip(q, x)], (8, OUT))
        trig = []
        for turns in (fx * (1.0 / 64.0), fy * (1.0 / 64.0), (fx + fy) * (1.0 / 64.0)):
            trig.append((sin_turns(turns + 0.25), sin_turns(turns)))
        for t, (cos, sin) in enumerate(trig):
            tab[1 + 2 * t, :, at] = cos
            tab[2 + 2 * t, :, at] = sin
        for half in range(REFS // 16):
            rows = slice(16 * half, 16 * half + 16)
            real, imag = refs[0, rows, at], refs[1, rows, at]
            shf[0, rows, at] = real
            shf[1, rows, at] = imag
            real, imag = real.astype(F32), imag.astype(F32)
            power = (real * real + imag * imag).astype(BF16) * BF16(-0.5)
            for t in range(TRANS):
                to = slice(t * REFS + 16 * half, t * REFS + 16 * half + 16)
                shf[2, to, at] = power
                if t:
                    cos, sin = twice(trig[t - 1][0]), twice(trig[t - 1][1])
                    shf[0, to, at] = (real * cos - imag * sin).astype(BF16)
                    shf[1, to, at] = (real * sin + imag * cos).astype(BF16)
        return 0

    lax.fori_loop(0, SY, tables_and_shifts, 0)

    def first_hop(o, _):
        swap_landed(o)
        ring_copy(0, 0, o).start()
        ring_copy(1, 0, o).start()
        core_copy(0, o).start()
        return 0

    lax.fori_loop(1, SX, first_hop, 0)

    def weigh(dist, o):
        core_landed(dist, o)
        block, src = lax.rem(z + dist, SZ), source(o)
        rows = pl.ds(pl.multiple_of(block * 64 + src * 16, 16), 16)
        tail = pl.ds(LOCAL, 128)
        d0 = gath[2 * block, src, :, tail].astype(F32)[:8]
        d1 = gath[2 * block + 1, src, :, tail].astype(F32)[:8]
        d = jnp.concatenate([d0, d1], axis=0)
        d = jnp.concatenate([d] * (PART // 128), axis=1)

        def part(k, _):
            at = pl.ds(pl.multiple_of(k * PART, PART), PART)
            transfer = sin_turns(twice(tab[0, :, at]) * d + PHASE) * (-AMP)
            fac = transfer * twice(tab[7, :, at])
            wgt[2, rows, at] = (fac * transfer).astype(BF16)
            a = gath[2 * block, src, :, at].astype(F32)
            b = gath[2 * block + 1, src, :, at].astype(F32)
            for comp in range(2):
                pick = slice(8 * comp, 8 * comp + 8)
                both = jnp.concatenate([a[pick], b[pick]], axis=0)
                wgt[comp, rows, at] = (both * fac).astype(BF16)
            return 0

        lax.fori_loop(0, LOCAL // PART, part, 0)

    def terms(dist):
        block = lax.rem(z + dist, SZ)
        rows = pl.ds(pl.multiple_of(block * 64, 64), 64)
        score[x, block] = (
            nt_dot(wgt[0, rows], shf[0]) + nt_dot(wgt[1, rows], shf[1])
            + nt_dot(wgt[2, rows], shf[2])
        )
        for o in range(1, SX):
            term_copy(dist, o).start()

    def own(o, _):
        weigh(0, o)
        return 0

    def event(e, _):
        step, o = e // SX, lax.rem(e, SX)
        for s in range(SZ // 2):

            @pl.when(step == s)
            def _():
                if s < 3:
                    for way in range(2):
                        ring_landed(way, s, o)
                    if s < 2:
                        for way in range(2):
                            ring_copy(way, s + 1, o).start()
                    else:

                        @pl.when(o < HALF)
                        def _():
                            ring_copy(0, 3, o).start()

                        @pl.when(o >= HALF)
                        def _():
                            ring_copy(1, 3, o).start()

                    core_copy(SZ - 1 - s, o).start()
                    core_copy(s + 1, o).start()
                else:

                    @pl.when(o < HALF)
                    def _():
                        ring_landed(0, 3, o)

                    @pl.when(o >= HALF)
                    def _():
                        ring_landed(1, 3, o)

                    core_copy(4, o).start()

        return 0

    def work(e):
        step, o = e // SX, lax.rem(e, SX)
        ways = 2 - step // 3

        def chunk(way, _):
            weigh((1 - way) * (SZ - 1 - step) + way * (step + 1), o)
            return 0

        lax.fori_loop(0, ways, chunk, 0)

        @pl.when(o == SX - 1)
        def _():
            def block(way, _):
                terms((1 - way) * (SZ - 1 - step) + way * (step + 1))
                return 0

            lax.fori_loop(0, ways, block, 0)

    def turn(e, _):
        event(e, None)

        @pl.when(e > 0)
        def _():
            work(e - 1)

        @pl.when(e == 0)
        def _():
            lax.fori_loop(0, SX, own, 0)
            terms(0)

        return 0

    lax.fori_loop(0, 4 * SX, turn, 0)
    work(4 * SX - 1)

    for dist in range(SZ):
        for o in range(1, SX):
            term_landed(dist, o)
    tops, totals = [], []
    for i in range(SZ // 2):
        rows = [
            (score[0, k] + score[1, k]) + (score[2, k] + score[3, k])
            for k in (2 * i, 2 * i + 1)
        ]
        turned = jnp.concatenate(rows, axis=0).T
        flip[:, i * 128 : (i + 1) * 128] = turned
        top = jnp.max(turned, axis=0, keepdims=True)
        tops.append(top)
        totals.append(jnp.sum(jnp.exp(turned - top), axis=0, keepdims=True))
    stat[me] = jnp.concatenate(tops + totals, axis=0)
    for step in range(1, 2 * SZ):
        stat_copy(step).start()
    for step in range(1, 2 * SZ):
        stat_landed(step)
    stats = stat[...]
    tops, totals = stats[:, 0:4], stats[:, 4:8]
    all_top = jnp.max(tops, axis=0)
    all_total = jnp.sum(totals * jnp.exp(tops - all_top[None]), axis=0)
    log_norm = all_top + jnp.log(all_total)
    for i in range(SZ // 2):
        at = slice(i * 128, (i + 1) * 128)
        posterior = jnp.exp(flip[:, at] - log_norm[i : i + 1]).astype(BF16)
        post[:, at] = posterior
        p = posterior.astype(F32)
        occ[:, at] = (
            p[0:REFS] + p[REFS : 2 * REFS] + p[2 * REFS : 3 * REFS] + p[3 * REFS :]
        ).astype(BF16)

    def y_step(i):
        return 4 + (1 - 2 * lax.rem(i, 2)) * ((i + 1) // 2)

    def y_copy(i):
        return remote(ysend.at[i], yrecv.at[i], ys_sem.at[i], yr_sem.at[i], y_mate(y_step(i)))

    def sums(i):
        at = local(lax.rem(y + y_step(i), SY))
        a0 = jnp.dot(post[...], wgt[0, :, at], preferred_element_type=F32)
        a1 = jnp.dot(post[...], wgt[1, :, at], preferred_element_type=F32)
        ctf = jnp.dot(occ[...], wgt[2, :, at], preferred_element_type=F32)
        real, imag = a0[0:REFS], a1[0:REFS]
        for t in range(1, TRANS):
            cos, sin = tab[2 * t - 1, :, at], tab[2 * t, :, at]
            cos = jnp.concatenate([cos] * (REFS // 8), axis=0)
            sin = jnp.concatenate([sin] * (REFS // 8), axis=0)
            b0, b1 = a0[t * REFS : (t + 1) * REFS], a1[t * REFS : (t + 1) * REFS]
            real = real + b0 * cos + b1 * sin
            imag = imag + b1 * cos - b0 * sin
        return real, imag, ctf

    def piece(i, _):
        real, imag, ctf = sums(i)

        @pl.when(i < SY - 1)
        def _():
            ysend[i, 0:REFS] = real.astype(BF16)
            ysend[i, REFS : 2 * REFS] = imag.astype(BF16)
            ysend[i, 2 * REFS :] = ctf.astype(BF16)
            y_copy(i).start()

        @pl.when(i == SY - 1)
        def _():
            total[0:REFS] = real
            total[REFS : 2 * REFS] = imag
            total[2 * REFS :] = ctf

        return 0

    lax.fori_loop(0, SY, piece, 0)

    def collect(i, _):
        y_copy(i).wait_recv()
        total[...] += yrecv[i].astype(F32)
        return 0

    lax.fori_loop(0, SY - 1, collect, 0)
    weight = total[2 * REFS :] + REGULARIZER
    out_ref[0] = total[0:REFS] / weight
    out_ref[1] = total[REFS : 2 * REFS] / weight

    def drain_ring(o, _):
        for s in range(3):
            for way in range(2):
                ring_copy(way, s, o).wait_send()

        @pl.when(o < HALF)
        def _():
            ring_copy(0, 3, o).wait_send()

        @pl.when(o >= HALF)
        def _():
            ring_copy(1, 3, o).wait_send()

        return 0

    lax.fori_loop(0, SX, drain_ring, 0)

    def drain_blocks(dist, _):
        for o in range(SX):
            core_copy(dist, o).wait_send()
        for o in range(1, SX):
            term_copy(dist, o).wait_send()
        return 0

    lax.fori_loop(0, SZ, drain_blocks, 0)

    def drain_swap(o, _):
        ref = gath.at[me, source(o)]
        remote(ref, ref, asend.at[o - 1], arecv.at[o - 1], x_mate(o)).wait_send()
        return 0

    lax.fori_loop(1, SX, drain_swap, 0)

    def drain_stats(step, _):
        stat_copy(step).wait_send()
        return 0

    lax.fori_loop(1, 2 * SZ, drain_stats, 0)

    def drain_sums(i, _):
        y_copy(i).wait_send()
        return 0

    lax.fori_loop(0, SY - 1, drain_sums, 0)


def shards(particles, defocus, references, noise_weights):
    dma = pltpu.SemaphoreType.DMA
    nblock = 2 * SZ
    rows = particles.shape[0] * particles.shape[1]
    vmem = pl.BlockSpec(memory_space=pltpu.VMEM)
    hbm = pl.BlockSpec(memory_space=pl.ANY)
    return pl.pallas_call(
        kernel,
        out_shape=jax.ShapeDtypeStruct((2, REFS, OUT), F32),
        in_specs=[hbm, vmem, hbm, vmem],
        out_specs=vmem,
        scratch_shapes=[
            pltpu.VMEM((nblock, SX, rows, WIDE), BF16),
            pltpu.VMEM((rows, 128), BF16),
            pltpu.VMEM((2, REFS, LOCAL), BF16),
            pltpu.VMEM((8, 8, LOCAL), F32),
            pltpu.VMEM((3, NPART, LOCAL), BF16),
            pltpu.VMEM((3, NREF, LOCAL), BF16),
            pltpu.VMEM((SX, SZ, 64, NREF), F32),
            pltpu.VMEM((nblock, 8, 128), F32),
            pltpu.VMEM((NREF, NPART), F32),
            pltpu.VMEM((NREF, NPART), BF16),
            pltpu.VMEM((REFS, NPART), BF16),
            pltpu.VMEM((SY - 1, 3 * REFS, OUT), BF16),
            pltpu.VMEM((SY - 1, 3 * REFS, OUT), BF16),
            pltpu.VMEM((3 * REFS, OUT), F32),
            dma,
            dma,
            dma((SX - 1,)),
            dma((SX - 1,)),
            dma((2, 4, SX)),
            dma((2, 4, SX)),
            dma((SZ, SX)),
            dma((SZ, SX)),
            dma((SZ, SX - 1)),
            dma((SZ, SX - 1)),
            dma((nblock - 1,)),
            dma((nblock - 1,)),
            dma((SY - 1,)),
            dma((SY - 1,)),
        ],
        name="expectation",
        compiler_params=pltpu.CompilerParams(
            collective_id=0, has_side_effects=True, vmem_limit_bytes=56 * 2**20
        ),
    )(
        particles.reshape(rows, PIX),
        defocus.reshape(1, 8),
        references,
        noise_weights.reshape(1, PIX),
    )


def solution(mesh):
    return jax.shard_map(
        shards,
        mesh=mesh,
        in_specs=(P(None, ("dom", "ref"), None), P(("dom", "ref")), P(None, "ref", None), P()),
        out_specs=P(None, "ref", "dom"),
        check_vma=False,
    )
```

```python
import jax
import jax.numpy as jnp
from jax import lax
from jax.experimental import pallas as pl
from jax.experimental.pallas import tpu as pltpu
from jax.sharding import PartitionSpec as P

PIX = 8192
TRANS = 4
REFS = 32
SX, SY, SZ = 4, 8, 8
OUT = 256
ROW = SX * OUT
LOCAL = SY * OUT
WIDE = LOCAL + 128
PART = 512
HALF = SX // 2
HALFZ = SZ // 2
NREF = TRANS * REFS
NPART = SZ * SX * 16
REGULARIZER = 0.05

AMP = 1.000012499921876
PHASE = 0.015941940272471127
INV_TWO_PI = 0.15915494309189535
SIN_TERMS = (
    6.283182818554191,
    -41.341421398928475,
    81.5961838781331,
    -76.58010057017961,
    41.205395033387106,
    -12.271262585212861,
)

MESH = pl.DeviceIdType.MESH
F32 = jnp.float32
BF16 = jnp.bfloat16


def sin_turns(turns):
    v = turns - jnp.round(turns)
    sq = v * v
    acc = sq * SIN_TERMS[5] + SIN_TERMS[4]
    for term in SIN_TERMS[3::-1]:
        acc = acc * sq + term
    return acc * v


def hop(o):
    return o + (o // 2) * (5 - 2 * o)


def nt_dot(a, b):
    return lax.dot_general(a, b, (((1,), (1,)), ((), ())), preferred_element_type=F32)


def twice(a):
    return jnp.concatenate([a, a], axis=0)


def kernel(
    part_ref, focus_ref, refs_ref, noise_ref, out_ref,
    gath, focus, few, refs, noise, tab, wgt, shf, score, stat, flip, post, occ, ysend, yrecv, total,
    local_sem, refs_sem, noise_sem, focus_sem, asend, arecv, ring_send, ring_recv, core_send, core_recv,
    tsend, trecv, lsend, lrecv, ssend, srecv, ys_sem, yr_sem,
):
    dom, me = lax.axis_index("dom"), lax.axis_index("ref")
    y, x, z, c = dom // SX, dom % SX, me // 2, me % 2
    other = (dom, z * 2 + 1 - c)
    up = (dom, lax.rem(z + 1, SZ) * 2 + c)
    down = (dom, lax.rem(z + SZ - 1, SZ) * 2 + c)

    def remote(src, dst, send, recv, device):
        return pltpu.make_async_remote_copy(
            src, dst, send, recv, device_id=device, device_id_type=MESH
        )

    def mate(step):
        return (dom, lax.rem(me + step, 2 * SZ))

    def x_mate(step):
        return (y * SX + lax.rem(x + step, SX), me)

    def y_mate(step):
        return (lax.rem(y + step, SY) * SX + x, me)

    def source(o):
        return lax.rem(x + SX - hop(o), SX)

    def strip(q, to):
        return pl.ds(pl.multiple_of(q * ROW + to * OUT, OUT), OUT)

    def local(q):
        return pl.ds(pl.multiple_of(q * OUT, OUT), OUT)

    for q in range(SY):
        pltpu.make_async_copy(
            part_ref.at[:, strip(q, x)], gath.at[me, x, :, local(q)], local_sem
        ).start()
    for q in range(SY):
        pltpu.make_async_copy(
            refs_ref.at[:, :, strip(q, x)], refs.at[:, :, local(q)], refs_sem
        ).start()
    for q in range(SY):
        pltpu.make_async_copy(
            noise_ref.at[:, strip(q, x)], noise.at[:, local(q)], noise_sem
        ).start()
    seen = pltpu.make_async_copy(focus_ref, few, focus_sem)
    seen.start()
    barrier = pltpu.get_barrier_semaphore()
    for step in range(1, 2 * SZ):
        pl.semaphore_signal(barrier, inc=1, device_id=mate(step), device_id_type=MESH)
    for step in range(1, SX):
        pl.semaphore_signal(barrier, inc=1, device_id=x_mate(step), device_id_type=MESH)
    for step in range(1, SY):
        pl.semaphore_signal(barrier, inc=1, device_id=y_mate(step), device_id_type=MESH)
    seen.wait()
    diagonal = lax.broadcasted_iota(jnp.int32, (8, 8), 0) == lax.broadcasted_iota(
        jnp.int32, (8, 8), 1
    )
    wide = jnp.broadcast_to(few[...].astype(F32), (8, 8))
    column = jnp.sum(jnp.where(diagonal, wide, 0.0), axis=1, keepdims=True)
    spread = twice(jnp.broadcast_to(column, (8, 128))).astype(BF16)
    focus[...] = spread
    gath[me, x, :, LOCAL:] = spread
    here = gath.at[me, x, :, pl.ds(0, LOCAL)]
    pltpu.make_async_copy(here, here, local_sem).wait()
    pl.semaphore_wait(barrier, 2 * SZ - 1 + SX - 1 + SY - 1)

    def ring_copy(way, step, o):
        block = lax.rem(z + SZ - step, SZ) if way == 0 else lax.rem(z + step, SZ)
        ref = gath.at[block * 2 + c, source(o)]
        return remote(
            ref, ref, ring_send.at[way, step, o], ring_recv.at[way, step, o],
            up if way == 0 else down,
        )

    def ring_landed(way, step, o):
        block = lax.rem(z + 2 * SZ - step - 1, SZ) if way == 0 else lax.rem(z + step + 1, SZ)
        ref = gath.at[block * 2 + c, source(o)]
        remote(
            ref, ref, ring_send.at[way, step, o], ring_recv.at[way, step, o],
            up if way == 0 else down,
        ).wait_recv()

    def core_copy(dist, o):
        ref = gath.at[lax.rem(z + dist, SZ) * 2 + c, source(o)]
        return remote(ref, ref, core_send.at[dist, o], core_recv.at[dist, o], other)

    def core_landed(dist, o):
        ref = gath.at[lax.rem(z + dist, SZ) * 2 + 1 - c, source(o)]
        remote(ref, ref, core_send.at[dist, o], core_recv.at[dist, o], other).wait_recv()

    def swap_landed(o):
        ref = gath.at[me, source(o)]
        remote(ref, ref, asend.at[o - 1], arecv.at[o - 1], x_mate(hop(o))).wait_recv()

    def term_copy(dist, o):
        ref = score.at[x, lax.rem(z + dist, SZ)]
        return remote(ref, ref, tsend.at[dist, o - 1], trecv.at[dist, o - 1], x_mate(hop(o)))

    def term_landed(dist, o):
        ref = score.at[source(o), lax.rem(z + dist, SZ)]
        remote(ref, ref, tsend.at[dist, o - 1], trecv.at[dist, o - 1], x_mate(hop(o))).wait_recv()

    def last_copy(u, o):
        at = pl.ds(pl.multiple_of(source(u) * 16, 16), 16)
        ref = score.at[x, lax.rem(z + HALFZ, SZ), at]
        return remote(ref, ref, lsend.at[u, o - 1], lrecv.at[u, o - 1], x_mate(hop(o)))

    def last_landed(u, o):
        row = lax.rem(source(o) + SX - hop(u), SX)
        at = pl.ds(pl.multiple_of(row * 16, 16), 16)
        ref = score.at[source(o), lax.rem(z + HALFZ, SZ), at]
        remote(ref, ref, lsend.at[u, o - 1], lrecv.at[u, o - 1], x_mate(hop(o))).wait_recv()

    def stat_copy(step):
        return remote(
            stat.at[me], stat.at[me], ssend.at[step - 1], srecv.at[step - 1], mate(step)
        )

    def stat_landed(step):
        ref = stat.at[lax.rem(me + 2 * SZ - step, 2 * SZ)]
        remote(ref, ref, ssend.at[step - 1], srecv.at[step - 1], mate(step)).wait_recv()

    ring_copy(0, 0, 0).start()
    ring_copy(1, 0, 0).start()
    for o in range(1, SX):
        to = lax.rem(x + hop(o), SX)
        for q in range(SY):
            remote(
                part_ref.at[:, strip(q, to)], gath.at[me, x, :, local(q)],
                asend.at[o - 1], arecv.at[o - 1], x_mate(hop(o)),
            ).start()
        remote(
            focus, gath.at[me, x, :, pl.ds(LOCAL, 128)],
            asend.at[o - 1], arecv.at[o - 1], x_mate(hop(o)),
        ).start()
    core_copy(0, 0).start()

    def tables_and_shifts(q, _):
        at = local(q)
        pixel = lax.broadcasted_iota(jnp.int32, (8, OUT), 1) + (q * ROW + x * OUT)
        fx = (lax.shift_right_logical(pixel, 6) - 64).astype(F32)
        fy = (pixel & 63).astype(F32)
        tab[0, :, at] = (fx * fx + fy * fy) * (INV_TWO_PI / 4096.0)
        tab[7, :, at] = jnp.broadcast_to(noise[:, at], (8, OUT))
        trig = []
        for turns in (fx * (1.0 / 64.0), fy * (1.0 / 64.0), (fx + fy) * (1.0 / 64.0)):
            trig.append((sin_turns(turns + 0.25), sin_turns(turns)))
        for t, (cos, sin) in enumerate(trig):
            tab[1 + 2 * t, :, at] = cos
            tab[2 + 2 * t, :, at] = sin
        for half in range(REFS // 16):
            rows = slice(16 * half, 16 * half + 16)
            real, imag = refs[0, rows, at], refs[1, rows, at]
            shf[0, rows, at] = real
            shf[1, rows, at] = imag
            real, imag = real.astype(F32), imag.astype(F32)
            power = (real * real + imag * imag).astype(BF16) * BF16(-0.5)
            for t in range(TRANS):
                to = slice(t * REFS + 16 * half, t * REFS + 16 * half + 16)
                shf[2, to, at] = power
                if t:
                    cos, sin = twice(trig[t - 1][0]), twice(trig[t - 1][1])
                    shf[0, to, at] = (real * cos - imag * sin).astype(BF16)
                    shf[1, to, at] = (real * sin + imag * cos).astype(BF16)
        return 0

    def first_hop(o, _):
        swap_landed(o)
        ring_copy(0, 0, o).start()
        ring_copy(1, 0, o).start()
        core_copy(0, o).start()
        return 0

    def weigh(dist, o):
        core_landed(dist, o)
        block, src = lax.rem(z + dist, SZ), source(o)
        rows = pl.ds(pl.multiple_of(block * 64 + src * 16, 16), 16)
        tail = pl.ds(LOCAL, 128)
        d0 = gath[2 * block, src, :, tail].astype(F32)[:8]
        d1 = gath[2 * block + 1, src, :, tail].astype(F32)[:8]
        d = jnp.concatenate([d0, d1], axis=0)
        d = jnp.concatenate([d] * (PART // 128), axis=1)

        def part(k, _):
            at = pl.ds(pl.multiple_of(k * PART, PART), PART)
            transfer = sin_turns(twice(tab[0, :, at]) * d + PHASE) * (-AMP)
            fac = transfer * twice(tab[7, :, at])
            wgt[2, rows, at] = (fac * transfer).astype(BF16)
            a = gath[2 * block, src, :, at].astype(F32)
            b = gath[2 * block + 1, src, :, at].astype(F32)
            for comp in range(2):
                pick = slice(8 * comp, 8 * comp + 8)
                both = jnp.concatenate([a[pick], b[pick]], axis=0)
                wgt[comp, rows, at] = (both * fac).astype(BF16)
            return 0

        lax.fori_loop(0, LOCAL // PART, part, 0)

    def dots(rows):
        return (
            nt_dot(wgt[0, rows], shf[0]) + nt_dot(wgt[1, rows], shf[1])
            + nt_dot(wgt[2, rows], shf[2])
        )

    def terms(dist):
        block = lax.rem(z + dist, SZ)
        score[x, block] = dots(pl.ds(pl.multiple_of(block * 64, 64), 64))
        for o in range(1, SX):
            term_copy(dist, o).start()

    def last_terms(u):
        at, block = pl.ds(pl.multiple_of(source(u) * 16, 16), 16), lax.rem(z + HALFZ, SZ)
        score[x, block, at] = dots(pl.ds(pl.multiple_of(block * 64 + source(u) * 16, 16), 16))
        for o in range(1, SX):
            last_copy(u, o).start()

    def own(o, _):
        weigh(0, o)
        return 0

    def chunk_of(e):
        k, last = lax.rem(e, SX), e // (3 * SX)
        return k + last * (lax.rem(k, HALF) * HALF + k // HALF - k)

    def event(e, _):
        step, o = e // SX, chunk_of(e)
        for s in range(SZ // 2):

            @pl.when(step == s)
            def _():
                if s < 3:
                    for way in range(2):
                        ring_landed(way, s, o)
                    if s < 2:
                        for way in range(2):
                            ring_copy(way, s + 1, o).start()
                    else:

                        @pl.when(o < HALF)
                        def _():
                            ring_copy(0, 3, o).start()

                        @pl.when(o >= HALF)
                        def _():
                            ring_copy(1, 3, o).start()

                    core_copy(SZ - 1 - s, o).start()
                    core_copy(s + 1, o).start()
                else:

                    @pl.when(o < HALF)
                    def _():
                        ring_landed(0, 3, o)

                    @pl.when(o >= HALF)
                    def _():
                        ring_landed(1, 3, o)

                    core_copy(4, o).start()

        return 0

    def work(e):
        step, o = e // SX, chunk_of(e)
        ways = 2 - step // 3

        def chunk(way, _):
            weigh((1 - way) * (SZ - 1 - step) + way * (step + 1), o)
            return 0

        lax.fori_loop(0, ways, chunk, 0)

        @pl.when(step == 3)
        def _():
            last_terms(o)

        @pl.when((step < 3) & (o == SX - 1))
        def _():
            def block(way, _):
                terms((1 - way) * (SZ - 1 - step) + way * (step + 1))
                return 0

            lax.fori_loop(0, ways, block, 0)

    def turn(e, _):
        event(e, None)
        work(e - 1)
        return 0

    event(0, None)
    lax.fori_loop(1, SX, first_hop, 0)
    pltpu.make_async_copy(refs, refs, refs_sem).wait()
    pltpu.make_async_copy(noise, noise, noise_sem).wait()
    lax.fori_loop(0, SY, tables_and_shifts, 0)
    lax.fori_loop(0, SX, own, 0)
    terms(0)
    lax.fori_loop(1, 4 * SX, turn, 0)
    work(4 * SX - 1)

    for dist in range(SZ):
        if dist != HALFZ:
            for o in range(1, SX):
                term_landed(dist, o)
    for u in range(SX):
        for o in range(1, SX):
            last_landed(u, o)
    tops, totals = [], []
    for i in range(SZ // 2):
        rows = [
            (score[0, k] + score[1, k]) + (score[2, k] + score[3, k])
            for k in (2 * i, 2 * i + 1)
        ]
        turned = jnp.concatenate(rows, axis=0).T
        flip[:, i * 128 : (i + 1) * 128] = turned
        top = jnp.max(turned, axis=0, keepdims=True)
        tops.append(top)
        totals.append(jnp.sum(jnp.exp(turned - top), axis=0, keepdims=True))
    stat[me] = jnp.concatenate(tops + totals, axis=0)
    for step in sorted(range(1, 2 * SZ), key=lambda k: abs(k - SZ)):
        stat_copy(step).start()
    for step in range(1, 2 * SZ):
        stat_landed(step)
    stats = stat[...]
    tops, totals = stats[:, 0:4], stats[:, 4:8]
    all_top = jnp.max(tops, axis=0)
    all_total = jnp.sum(totals * jnp.exp(tops - all_top[None]), axis=0)
    log_norm = all_top + jnp.log(all_total)
    for i in range(SZ // 2):
        at = slice(i * 128, (i + 1) * 128)
        posterior = jnp.exp(flip[:, at] - log_norm[i : i + 1]).astype(BF16)
        post[:, at] = posterior
        p = posterior.astype(F32)
        occ[:, at] = (
            p[0:REFS] + p[REFS : 2 * REFS] + p[2 * REFS : 3 * REFS] + p[3 * REFS :]
        ).astype(BF16)

    def y_step(i):
        return 4 + (1 - 2 * lax.rem(i, 2)) * ((i + 1) // 2)

    def y_copy(i):
        return remote(ysend.at[i], yrecv.at[i], ys_sem.at[i], yr_sem.at[i], y_mate(y_step(i)))

    def sums(i):
        at = local(lax.rem(y + y_step(i), SY))
        a0 = jnp.dot(post[...], wgt[0, :, at], preferred_element_type=F32)
        a1 = jnp.dot(post[...], wgt[1, :, at], preferred_element_type=F32)
        ctf = jnp.dot(occ[...], wgt[2, :, at], preferred_element_type=F32)
        real, imag = a0[0:REFS], a1[0:REFS]
        for t in range(1, TRANS):
            cos, sin = tab[2 * t - 1, :, at], tab[2 * t, :, at]
            cos = jnp.concatenate([cos] * (REFS // 8), axis=0)
            sin = jnp.concatenate([sin] * (REFS // 8), axis=0)
            b0, b1 = a0[t * REFS : (t + 1) * REFS], a1[t * REFS : (t + 1) * REFS]
            real = real + b0 * cos + b1 * sin
            imag = imag + b1 * cos - b0 * sin
        return real, imag, ctf

    def piece(i, _):
        real, imag, ctf = sums(i)

        @pl.when(i < SY - 1)
        def _():
            ysend[i, 0:REFS] = real.astype(BF16)
            ysend[i, REFS : 2 * REFS] = imag.astype(BF16)
            ysend[i, 2 * REFS :] = ctf.astype(BF16)
            y_copy(i).start()

        @pl.when(i == SY - 1)
        def _():
            total[0:REFS] = real
            total[REFS : 2 * REFS] = imag
            total[2 * REFS :] = ctf

        return 0

    lax.fori_loop(0, SY, piece, 0)

    def collect(i, _):
        y_copy(i).wait_recv()
        total[...] += yrecv[i].astype(F32)
        return 0

    lax.fori_loop(0, SY - 1, collect, 0)
    weight = total[2 * REFS :] + REGULARIZER
    out_ref[0] = total[0:REFS] / weight
    out_ref[1] = total[REFS : 2 * REFS] / weight

    def drain_ring(o, _):
        for s in range(3):
            for way in range(2):
                ring_copy(way, s, o).wait_send()

        @pl.when(o < HALF)
        def _():
            ring_copy(0, 3, o).wait_send()

        @pl.when(o >= HALF)
        def _():
            ring_copy(1, 3, o).wait_send()

        return 0

    lax.fori_loop(0, SX, drain_ring, 0)

    def drain_blocks(dist, _):
        for o in range(SX):
            core_copy(dist, o).wait_send()

        @pl.when(dist != HALFZ)
        def _():
            for o in range(1, SX):
                term_copy(dist, o).wait_send()

        return 0

    lax.fori_loop(0, SZ, drain_blocks, 0)

    def drain_last(u, _):
        for o in range(1, SX):
            last_copy(u, o).wait_send()
        return 0

    lax.fori_loop(0, SX, drain_last, 0)

    def drain_swap(o, _):
        ref = gath.at[me, source(o)]
        remote(ref, ref, asend.at[o - 1], arecv.at[o - 1], x_mate(hop(o))).wait_send()
        return 0

    lax.fori_loop(1, SX, drain_swap, 0)

    def drain_stats(step, _):
        stat_copy(step).wait_send()
        return 0

    lax.fori_loop(1, 2 * SZ, drain_stats, 0)

    def drain_sums(i, _):
        y_copy(i).wait_send()
        return 0

    lax.fori_loop(0, SY - 1, drain_sums, 0)


def shards(particles, defocus, references, noise_weights):
    dma = pltpu.SemaphoreType.DMA
    nblock = 2 * SZ
    rows = particles.shape[0] * particles.shape[1]
    vmem = pl.BlockSpec(memory_space=pltpu.VMEM)
    hbm = pl.BlockSpec(memory_space=pl.ANY)
    return pl.pallas_call(
        kernel,
        out_shape=pltpu.VMEM((2, REFS, OUT), F32),
        in_specs=[hbm, hbm, hbm, hbm],
        out_specs=vmem,
        scratch_shapes=[
            pltpu.VMEM((nblock, SX, rows, WIDE), BF16),
            pltpu.VMEM((rows, 128), BF16),
            pltpu.VMEM((1, 8), BF16),
            pltpu.VMEM((2, REFS, LOCAL), BF16),
            pltpu.VMEM((1, LOCAL), F32),
            pltpu.VMEM((8, 8, LOCAL), F32),
            pltpu.VMEM((3, NPART, LOCAL), BF16),
            pltpu.VMEM((3, NREF, LOCAL), BF16),
            pltpu.VMEM((SX, SZ, 64, NREF), F32),
            pltpu.VMEM((nblock, 8, 128), F32),
            pltpu.VMEM((NREF, NPART), F32),
            pltpu.VMEM((NREF, NPART), BF16),
            pltpu.VMEM((REFS, NPART), BF16),
            pltpu.VMEM((SY - 1, 3 * REFS, OUT), BF16),
            pltpu.VMEM((SY - 1, 3 * REFS, OUT), BF16),
            pltpu.VMEM((3 * REFS, OUT), F32),
            dma,
            dma,
            dma,
            dma,
            dma((SX - 1,)),
            dma((SX - 1,)),
            dma((2, 4, SX)),
            dma((2, 4, SX)),
            dma((SZ, SX)),
            dma((SZ, SX)),
            dma((SZ, SX - 1)),
            dma((SZ, SX - 1)),
            dma((SX, SX - 1)),
            dma((SX, SX - 1)),
            dma((nblock - 1,)),
            dma((nblock - 1,)),
            dma((SY - 1,)),
            dma((SY - 1,)),
        ],
        name="expectation",
        compiler_params=pltpu.CompilerParams(
            collective_id=0, has_side_effects=True, vmem_limit_bytes=56 * 2**20
        ),
    )(
        particles.reshape(rows, PIX),
        defocus.reshape(1, 8),
        references,
        noise_weights.reshape(1, PIX),
    )


def solution(mesh):
    return jax.shard_map(
        shards,
        mesh=mesh,
        in_specs=(P(None, ("dom", "ref"), None), P(("dom", "ref")), P(None, "ref", None), P()),
        out_specs=P(None, "ref", "dom"),
        check_vma=False,
    )
```

```python
import jax
import jax.numpy as jnp
from jax import lax
from jax.experimental import pallas as pl
from jax.experimental.pallas import tpu as pltpu
from jax.sharding import PartitionSpec as P

PIX = 8192
TRANS = 4
REFS = 32
SX, SY, SZ = 4, 8, 8
OUT = 256
ROW = SX * OUT
LOCAL = SY * OUT
WIDE = LOCAL + 128
PART = 512
HALF = SX // 2
HALFZ = SZ // 2
NREF = TRANS * REFS
MID = 3 * REFS // 2
NPART = SZ * SX * 16
REGULARIZER = 0.05

AMP = 1.000012499921876
PHASE = 0.015941940272471127
INV_TWO_PI = 0.15915494309189535
SIN_TERMS = (
    6.283182818554191,
    -41.341421398928475,
    81.5961838781331,
    -76.58010057017961,
    41.205395033387106,
    -12.271262585212861,
)

MESH = pl.DeviceIdType.MESH
F32 = jnp.float32
BF16 = jnp.bfloat16


def sin_turns(turns):
    v = turns - jnp.round(turns)
    sq = v * v
    acc = sq * SIN_TERMS[5] + SIN_TERMS[4]
    for term in SIN_TERMS[3::-1]:
        acc = acc * sq + term
    return acc * v


def hop(o):
    return o + (o // 2) * (5 - 2 * o)


def nt_dot(a, b):
    return lax.dot_general(a, b, (((1,), (1,)), ((), ())), preferred_element_type=F32)


def twice(a):
    return jnp.concatenate([a, a], axis=0)


def kernel(
    part_ref, focus_ref, refs_ref, noise_ref, out_ref,
    gath, focus, few, refs, noise, tab, wgt, shf, score, stat, flip, post, occ, ysend, yrecv, hold, total,
    local_sem, refs_sem, noise_sem, focus_sem, asend, arecv, ring_send, ring_recv, core_send, core_recv,
    tsend, trecv, lsend, lrecv, ssend, srecv, ys_sem, yr_sem,
):
    dom, me = lax.axis_index("dom"), lax.axis_index("ref")
    y, x, z, c = dom // SX, dom % SX, me // 2, me % 2
    other = (dom, z * 2 + 1 - c)
    up = (dom, lax.rem(z + 1, SZ) * 2 + c)
    down = (dom, lax.rem(z + SZ - 1, SZ) * 2 + c)

    def remote(src, dst, send, recv, device):
        return pltpu.make_async_remote_copy(
            src, dst, send, recv, device_id=device, device_id_type=MESH
        )

    def mate(step):
        return (dom, lax.rem(me + step, 2 * SZ))

    def x_mate(step):
        return (y * SX + lax.rem(x + step, SX), me)

    def y_mate(step):
        return (lax.rem(y + step, SY) * SX + x, me)

    def source(o):
        return lax.rem(x + SX - hop(o), SX)

    def strip(q, to):
        return pl.ds(pl.multiple_of(q * ROW + to * OUT, OUT), OUT)

    def local(q):
        return pl.ds(pl.multiple_of(q * OUT, OUT), OUT)

    for q in range(SY):
        pltpu.make_async_copy(
            part_ref.at[:, strip(q, x)], gath.at[me, x, :, local(q)], local_sem
        ).start()
    for q in range(SY):
        pltpu.make_async_copy(
            refs_ref.at[:, :, strip(q, x)], refs.at[:, :, local(q)], refs_sem
        ).start()
    for q in range(SY):
        pltpu.make_async_copy(
            noise_ref.at[:, strip(q, x)], noise.at[:, local(q)], noise_sem
        ).start()
    seen = pltpu.make_async_copy(focus_ref, few, focus_sem)
    seen.start()
    barrier = pltpu.get_barrier_semaphore()
    for step in range(1, 2 * SZ):
        pl.semaphore_signal(barrier, inc=1, device_id=mate(step), device_id_type=MESH)
    for step in range(1, SX):
        pl.semaphore_signal(barrier, inc=1, device_id=x_mate(step), device_id_type=MESH)
    for step in range(1, SY):
        pl.semaphore_signal(barrier, inc=1, device_id=y_mate(step), device_id_type=MESH)
    seen.wait()
    diagonal = lax.broadcasted_iota(jnp.int32, (8, 8), 0) == lax.broadcasted_iota(
        jnp.int32, (8, 8), 1
    )
    wide = jnp.broadcast_to(few[...].astype(F32), (8, 8))
    column = jnp.sum(jnp.where(diagonal, wide, 0.0), axis=1, keepdims=True)
    spread = twice(jnp.broadcast_to(column, (8, 128))).astype(BF16)
    focus[...] = spread
    gath[me, x, :, LOCAL:] = spread
    here = gath.at[me, x, :, pl.ds(0, LOCAL)]
    pltpu.make_async_copy(here, here, local_sem).wait()
    pl.semaphore_wait(barrier, 2 * SZ - 1 + SX - 1 + SY - 1)

    def ring_copy(way, step, o):
        block = lax.rem(z + SZ - step, SZ) if way == 0 else lax.rem(z + step, SZ)
        ref = gath.at[block * 2 + c, source(o)]
        return remote(
            ref, ref, ring_send.at[way, step, o], ring_recv.at[way, step, o],
            up if way == 0 else down,
        )

    def ring_landed(way, step, o):
        block = lax.rem(z + 2 * SZ - step - 1, SZ) if way == 0 else lax.rem(z + step + 1, SZ)
        ref = gath.at[block * 2 + c, source(o)]
        remote(
            ref, ref, ring_send.at[way, step, o], ring_recv.at[way, step, o],
            up if way == 0 else down,
        ).wait_recv()

    def core_copy(dist, o):
        ref = gath.at[lax.rem(z + dist, SZ) * 2 + c, source(o)]
        return remote(ref, ref, core_send.at[dist, o], core_recv.at[dist, o], other)

    def core_landed(dist, o):
        ref = gath.at[lax.rem(z + dist, SZ) * 2 + 1 - c, source(o)]
        remote(ref, ref, core_send.at[dist, o], core_recv.at[dist, o], other).wait_recv()

    def swap_landed(o):
        ref = gath.at[me, source(o)]
        remote(ref, ref, asend.at[o - 1], arecv.at[o - 1], x_mate(hop(o))).wait_recv()

    def term_copy(dist, o):
        ref = score.at[x, lax.rem(z + dist, SZ)]
        return remote(ref, ref, tsend.at[dist, o - 1], trecv.at[dist, o - 1], x_mate(hop(o)))

    def term_landed(dist, o):
        ref = score.at[source(o), lax.rem(z + dist, SZ)]
        remote(ref, ref, tsend.at[dist, o - 1], trecv.at[dist, o - 1], x_mate(hop(o))).wait_recv()

    def last_copy(u, o):
        at = pl.ds(pl.multiple_of(source(u) * 16, 16), 16)
        ref = score.at[x, lax.rem(z + HALFZ, SZ), at]
        return remote(ref, ref, lsend.at[u, o - 1], lrecv.at[u, o - 1], x_mate(hop(o)))

    def last_landed(u, o):
        row = lax.rem(source(o) + SX - hop(u), SX)
        at = pl.ds(pl.multiple_of(row * 16, 16), 16)
        ref = score.at[source(o), lax.rem(z + HALFZ, SZ), at]
        remote(ref, ref, lsend.at[u, o - 1], lrecv.at[u, o - 1], x_mate(hop(o))).wait_recv()

    def stat_copy(step):
        return remote(
            stat.at[me], stat.at[me], ssend.at[step - 1], srecv.at[step - 1], mate(step)
        )

    def stat_landed(step):
        ref = stat.at[lax.rem(me + 2 * SZ - step, 2 * SZ)]
        remote(ref, ref, ssend.at[step - 1], srecv.at[step - 1], mate(step)).wait_recv()

    ring_copy(0, 0, 0).start()
    ring_copy(1, 0, 0).start()
    for o in range(1, SX):
        to = lax.rem(x + hop(o), SX)
        for q in range(SY):
            remote(
                part_ref.at[:, strip(q, to)], gath.at[me, x, :, local(q)],
                asend.at[o - 1], arecv.at[o - 1], x_mate(hop(o)),
            ).start()
        remote(
            focus, gath.at[me, x, :, pl.ds(LOCAL, 128)],
            asend.at[o - 1], arecv.at[o - 1], x_mate(hop(o)),
        ).start()
    core_copy(0, 0).start()

    def tables_and_shifts(q, _):
        at = local(q)
        pixel = lax.broadcasted_iota(jnp.int32, (8, OUT), 1) + (q * ROW + x * OUT)
        fx = (lax.shift_right_logical(pixel, 6) - 64).astype(F32)
        fy = (pixel & 63).astype(F32)
        tab[0, :, at] = (fx * fx + fy * fy) * (INV_TWO_PI / 4096.0)
        tab[7, :, at] = jnp.broadcast_to(noise[:, at], (8, OUT))
        trig = []
        for turns in (fx * (1.0 / 64.0), fy * (1.0 / 64.0), (fx + fy) * (1.0 / 64.0)):
            trig.append((sin_turns(turns + 0.25), sin_turns(turns)))
        for t, (cos, sin) in enumerate(trig):
            tab[1 + 2 * t, :, at] = cos
            tab[2 + 2 * t, :, at] = sin
        for half in range(REFS // 16):
            rows = slice(16 * half, 16 * half + 16)
            real, imag = refs[0, rows, at], refs[1, rows, at]
            shf[0, rows, at] = real
            shf[1, rows, at] = imag
            real, imag = real.astype(F32), imag.astype(F32)
            power = (real * real + imag * imag).astype(BF16) * BF16(-0.5)
            for t in range(TRANS):
                to = slice(t * REFS + 16 * half, t * REFS + 16 * half + 16)
                shf[2, to, at] = power
                if t:
                    cos, sin = twice(trig[t - 1][0]), twice(trig[t - 1][1])
                    shf[0, to, at] = (real * cos - imag * sin).astype(BF16)
                    shf[1, to, at] = (real * sin + imag * cos).astype(BF16)
        return 0

    def first_hop(o, _):
        swap_landed(o)
        ring_copy(0, 0, o).start()
        ring_copy(1, 0, o).start()
        core_copy(0, o).start()
        return 0

    def weigh(dist, o):
        core_landed(dist, o)
        block, src = lax.rem(z + dist, SZ), source(o)
        rows = pl.ds(pl.multiple_of(block * 64 + src * 16, 16), 16)
        tail = pl.ds(LOCAL, 128)
        d0 = gath[2 * block, src, :, tail].astype(F32)[:8]
        d1 = gath[2 * block + 1, src, :, tail].astype(F32)[:8]
        d = jnp.concatenate([d0, d1], axis=0)
        d = jnp.concatenate([d] * (PART // 128), axis=1)

        def part(k, _):
            at = pl.ds(pl.multiple_of(k * PART, PART), PART)
            transfer = sin_turns(twice(tab[0, :, at]) * d + PHASE) * (-AMP)
            fac = transfer * twice(tab[7, :, at])
            wgt[2, rows, at] = (fac * transfer).astype(BF16)
            a = gath[2 * block, src, :, at].astype(F32)
            b = gath[2 * block + 1, src, :, at].astype(F32)
            for comp in range(2):
                pick = slice(8 * comp, 8 * comp + 8)
                both = jnp.concatenate([a[pick], b[pick]], axis=0)
                wgt[comp, rows, at] = (both * fac).astype(BF16)
            return 0

        lax.fori_loop(0, LOCAL // PART, part, 0)

    def dots(rows):
        return (
            nt_dot(wgt[0, rows], shf[0]) + nt_dot(wgt[1, rows], shf[1])
            + nt_dot(wgt[2, rows], shf[2])
        )

    def terms(dist):
        block = lax.rem(z + dist, SZ)
        score[x, block] = dots(pl.ds(pl.multiple_of(block * 64, 64), 64))
        for o in range(1, SX):
            term_copy(dist, o).start()

    def last_terms(u):
        at, block = pl.ds(pl.multiple_of(source(u) * 16, 16), 16), lax.rem(z + HALFZ, SZ)
        score[x, block, at] = dots(pl.ds(pl.multiple_of(block * 64 + source(u) * 16, 16), 16))
        for o in range(1, SX):
            last_copy(u, o).start()

    def own(o, _):
        weigh(0, o)
        return 0

    def chunk_of(e):
        k, last = lax.rem(e, SX), e // (3 * SX)
        return k + last * (lax.rem(k, HALF) * HALF + k // HALF - k)

    def event(e, _):
        step, o = e // SX, chunk_of(e)
        for s in range(SZ // 2):

            @pl.when(step == s)
            def _():
                if s < 3:
                    for way in range(2):
                        ring_landed(way, s, o)
                    if s < 2:
                        for way in range(2):
                            ring_copy(way, s + 1, o).start()
                    else:

                        @pl.when(o < HALF)
                        def _():
                            ring_copy(0, 3, o).start()

                        @pl.when(o >= HALF)
                        def _():
                            ring_copy(1, 3, o).start()

                    core_copy(SZ - 1 - s, o).start()
                    core_copy(s + 1, o).start()
                else:

                    @pl.when(o < HALF)
                    def _():
                        ring_landed(0, 3, o)

                    @pl.when(o >= HALF)
                    def _():
                        ring_landed(1, 3, o)

                    core_copy(4, o).start()

        return 0

    def work(e):
        step, o = e // SX, chunk_of(e)
        ways = 2 - step // 3

        def chunk(way, _):
            weigh((1 - way) * (SZ - 1 - step) + way * (step + 1), o)
            return 0

        lax.fori_loop(0, ways, chunk, 0)

        @pl.when(step == 3)
        def _():
            last_terms(o)

        @pl.when((step < 3) & (o == SX - 1))
        def _():
            def block(way, _):
                terms((1 - way) * (SZ - 1 - step) + way * (step + 1))
                return 0

            lax.fori_loop(0, ways, block, 0)

    def turn(e, _):
        event(e, None)
        work(e - 1)
        return 0

    event(0, None)
    lax.fori_loop(1, SX, first_hop, 0)
    pltpu.make_async_copy(refs, refs, refs_sem).wait()
    pltpu.make_async_copy(noise, noise, noise_sem).wait()
    lax.fori_loop(0, SY, tables_and_shifts, 0)
    lax.fori_loop(0, SX, own, 0)
    terms(0)
    lax.fori_loop(1, 4 * SX, turn, 0)
    work(4 * SX - 1)

    for dist in range(SZ):
        if dist != HALFZ:
            for o in range(1, SX):
                term_landed(dist, o)
    for u in range(SX):
        for o in range(1, SX):
            last_landed(u, o)
    tops, totals = [], []
    for i in range(SZ // 2):
        rows = [
            (score[0, k] + score[1, k]) + (score[2, k] + score[3, k])
            for k in (2 * i, 2 * i + 1)
        ]
        turned = jnp.concatenate(rows, axis=0).T
        flip[:, i * 128 : (i + 1) * 128] = turned
        top = jnp.max(turned, axis=0, keepdims=True)
        tops.append(top)
        totals.append(jnp.sum(jnp.exp(turned - top), axis=0, keepdims=True))
    stat[me] = jnp.concatenate(tops + totals, axis=0)
    for step in sorted(range(1, 2 * SZ), key=lambda k: abs(k - SZ)):
        stat_copy(step).start()
    for step in range(1, 2 * SZ):
        stat_landed(step)
    stats = stat[...]
    tops, totals = stats[:, 0:4], stats[:, 4:8]
    all_top = jnp.max(tops, axis=0)
    all_total = jnp.sum(totals * jnp.exp(tops - all_top[None]), axis=0)
    log_norm = all_top + jnp.log(all_total)
    for i in range(SZ // 2):
        at = slice(i * 128, (i + 1) * 128)
        posterior = jnp.exp(flip[:, at] - log_norm[i : i + 1]).astype(BF16)
        post[:, at] = posterior
        p = posterior.astype(F32)
        occ[:, at] = (
            p[0:REFS] + p[REFS : 2 * REFS] + p[2 * REFS : 3 * REFS] + p[3 * REFS :]
        ).astype(BF16)

    def y_step(i):
        j = (i + 1) // 2
        return 4 - j + 2 * j * lax.rem(i + 1, 2)

    top_half, low_half = slice(0, MID), slice(MID, 2 * MID)

    def y_copy(i, step, rows=slice(0, 2 * MID), sem=None):
        sem = i if sem is None else sem
        return remote(
            ysend.at[i, rows], yrecv.at[i, rows], ys_sem.at[sem], yr_sem.at[sem], y_mate(step)
        )

    def y_copies():
        return (
            y_copy(0, 2, top_half), y_copy(1, 1), y_copy(2, SY - 1), y_copy(3, 2),
            y_copy(4, SY - 2), y_copy(5, 1), y_copy(6, SY - 1), y_copy(0, SY - 2, low_half, 7),
        )

    def sums(i):
        at = local(lax.rem(y + y_step(i), SY))
        a0 = jnp.dot(post[...], wgt[0, :, at], preferred_element_type=F32)
        a1 = jnp.dot(post[...], wgt[1, :, at], preferred_element_type=F32)
        ctf = jnp.dot(occ[...], wgt[2, :, at], preferred_element_type=F32)
        real, imag = a0[0:REFS], a1[0:REFS]
        for t in range(1, TRANS):
            cos, sin = tab[2 * t - 1, :, at], tab[2 * t, :, at]
            cos = jnp.concatenate([cos] * (REFS // 8), axis=0)
            sin = jnp.concatenate([sin] * (REFS // 8), axis=0)
            b0, b1 = a0[t * REFS : (t + 1) * REFS], a1[t * REFS : (t + 1) * REFS]
            real = real + b0 * cos + b1 * sin
            imag = imag + b1 * cos - b0 * sin
        return real, imag, ctf

    def piece(i, _):
        real, imag, ctf = sums(i)

        @pl.when((i < 3) | (i == 5) | (i == 6))
        def _():
            ysend[i, 0:REFS] = real.astype(BF16)
            ysend[i, REFS : 2 * REFS] = imag.astype(BF16)
            ysend[i, 2 * REFS :] = ctf.astype(BF16)

        @pl.when((i == 3) | (i == 4))
        def _():
            hold[i - 3, 0:REFS] = real
            hold[i - 3, REFS : 2 * REFS] = imag
            hold[i - 3, 2 * REFS :] = ctf

        @pl.when(i == SY - 1)
        def _():
            total[0:REFS] = real
            total[REFS : 2 * REFS] = imag
            total[2 * REFS :] = ctf

        for k in (0, 1, 2, 5, 6):

            @pl.when(i == k)
            def _():
                y_copies()[k].start()
                if k == 0:
                    y_copies()[7].start()

        return 0

    lax.fori_loop(0, SY, piece, 0)

    near, far = y_copies()[1], y_copies()[0]
    near.wait_recv()
    far.wait_recv()
    both = hold[0] + yrecv[1].astype(F32)
    ysend[3, top_half] = (both[top_half] + yrecv[0, top_half].astype(F32)).astype(BF16)
    ysend[3, low_half] = both[low_half].astype(BF16)
    y_copies()[3].start()
    near, far = y_copies()[2], y_copies()[7]
    near.wait_recv()
    far.wait_recv()
    both = hold[1] + yrecv[2].astype(F32)
    ysend[4, top_half] = both[top_half].astype(BF16)
    ysend[4, low_half] = (both[low_half] + yrecv[0, low_half].astype(F32)).astype(BF16)
    y_copies()[4].start()

    y_copies()[5].wait_recv()
    y_copies()[6].wait_recv()
    total[...] += yrecv[5].astype(F32) + yrecv[6].astype(F32)
    y_copies()[3].wait_recv()
    y_copies()[4].wait_recv()
    total[...] += yrecv[3].astype(F32) + yrecv[4].astype(F32)
    weight = total[2 * REFS :] + REGULARIZER
    out_ref[0] = total[0:REFS] / weight
    out_ref[1] = total[REFS : 2 * REFS] / weight

    def drain_ring(o, _):
        for s in range(3):
            for way in range(2):
                ring_copy(way, s, o).wait_send()

        @pl.when(o < HALF)
        def _():
            ring_copy(0, 3, o).wait_send()

        @pl.when(o >= HALF)
        def _():
            ring_copy(1, 3, o).wait_send()

        return 0

    lax.fori_loop(0, SX, drain_ring, 0)

    def drain_blocks(dist, _):
        for o in range(SX):
            core_copy(dist, o).wait_send()

        @pl.when(dist != HALFZ)
        def _():
            for o in range(1, SX):
                term_copy(dist, o).wait_send()

        return 0

    lax.fori_loop(0, SZ, drain_blocks, 0)

    def drain_last(u, _):
        for o in range(1, SX):
            last_copy(u, o).wait_send()
        return 0

    lax.fori_loop(0, SX, drain_last, 0)

    def drain_swap(o, _):
        ref = gath.at[me, source(o)]
        remote(ref, ref, asend.at[o - 1], arecv.at[o - 1], x_mate(hop(o))).wait_send()
        return 0

    lax.fori_loop(1, SX, drain_swap, 0)

    def drain_stats(step, _):
        stat_copy(step).wait_send()
        return 0

    lax.fori_loop(1, 2 * SZ, drain_stats, 0)

    for copy in y_copies():
        copy.wait_send()


def shards(particles, defocus, references, noise_weights):
    dma = pltpu.SemaphoreType.DMA
    nblock = 2 * SZ
    rows = particles.shape[0] * particles.shape[1]
    vmem = pl.BlockSpec(memory_space=pltpu.VMEM)
    hbm = pl.BlockSpec(memory_space=pl.ANY)
    return pl.pallas_call(
        kernel,
        out_shape=pltpu.VMEM((2, REFS, OUT), F32),
        in_specs=[hbm, hbm, hbm, hbm],
        out_specs=vmem,
        scratch_shapes=[
            pltpu.VMEM((nblock, SX, rows, WIDE), BF16),
            pltpu.VMEM((rows, 128), BF16),
            pltpu.VMEM((1, 8), BF16),
            pltpu.VMEM((2, REFS, LOCAL), BF16),
            pltpu.VMEM((1, LOCAL), F32),
            pltpu.VMEM((8, 8, LOCAL), F32),
            pltpu.VMEM((3, NPART, LOCAL), BF16),
            pltpu.VMEM((3, NREF, LOCAL), BF16),
            pltpu.VMEM((SX, SZ, 64, NREF), F32),
            pltpu.VMEM((nblock, 8, 128), F32),
            pltpu.VMEM((NREF, NPART), F32),
            pltpu.VMEM((NREF, NPART), BF16),
            pltpu.VMEM((REFS, NPART), BF16),
            pltpu.VMEM((SY - 1, 3 * REFS, OUT), BF16),
            pltpu.VMEM((SY - 1, 3 * REFS, OUT), BF16),
            pltpu.VMEM((2, 3 * REFS, OUT), F32),
            pltpu.VMEM((3 * REFS, OUT), F32),
            dma,
            dma,
            dma,
            dma,
            dma((SX - 1,)),
            dma((SX - 1,)),
            dma((2, 4, SX)),
            dma((2, 4, SX)),
            dma((SZ, SX)),
            dma((SZ, SX)),
            dma((SZ, SX - 1)),
            dma((SZ, SX - 1)),
            dma((SX, SX - 1)),
            dma((SX, SX - 1)),
            dma((nblock - 1,)),
            dma((nblock - 1,)),
            dma((SY,)),
            dma((SY,)),
        ],
        name="expectation",
        compiler_params=pltpu.CompilerParams(
            collective_id=0, has_side_effects=True, vmem_limit_bytes=56 * 2**20
        ),
    )(
        particles.reshape(rows, PIX),
        defocus.reshape(1, 8),
        references,
        noise_weights.reshape(1, PIX),
    )


def solution(mesh):
    return jax.shard_map(
        shards,
        mesh=mesh,
        in_specs=(P(None, ("dom", "ref"), None), P(("dom", "ref")), P(None, "ref", None), P()),
        out_specs=P(None, "ref", "dom"),
        check_vma=False,
    )
```

```python
import jax
import jax.numpy as jnp
from jax import lax
from jax.experimental import pallas as pl
from jax.experimental.pallas import tpu as pltpu
from jax.sharding import PartitionSpec as P

PIX = 8192
TRANS = 4
REFS = 32
SX, SY, SZ = 4, 8, 8
OUT = 256
ROW = SX * OUT
LOCAL = SY * OUT
WIDE = LOCAL + 128
PART = 512
HALF = SX // 2
HALFZ = SZ // 2
NREF = TRANS * REFS
MID = 3 * REFS // 2
NPART = SZ * SX * 16
REGULARIZER = 0.05

AMP = 1.000012499921876
PHASE = 0.015941940272471127
INV_TWO_PI = 0.15915494309189535
SIN_TERMS = (
    6.283182818554191,
    -41.341421398928475,
    81.5961838781331,
    -76.58010057017961,
    41.205395033387106,
    -12.271262585212861,
)

MESH = pl.DeviceIdType.MESH
F32 = jnp.float32
BF16 = jnp.bfloat16


def sin_turns(turns):
    v = turns - jnp.round(turns)
    sq = v * v
    acc = sq * SIN_TERMS[5] + SIN_TERMS[4]
    for term in SIN_TERMS[3::-1]:
        acc = acc * sq + term
    return acc * v


def hop(o):
    return o + (o // 2) * (5 - 2 * o)


def twice(a):
    return jnp.concatenate([a, a], axis=0)


def kernel(
    part_ref, focus_ref, refs_ref, noise_ref, out_ref,
    gath, focus, few, refs, noise, tab, wgt, shf, turned, score, stat, flip, post, occ, ysend, yrecv, hold, total,
    local_sem, refs_sem, noise_sem, focus_sem, asend, arecv, ring_send, ring_recv, core_send, core_recv,
    tsend, trecv, lsend, lrecv, ssend, srecv, ys_sem, yr_sem,
):
    dom, me = lax.axis_index("dom"), lax.axis_index("ref")
    y, x, z, c = dom // SX, dom % SX, me // 2, me % 2
    other = (dom, z * 2 + 1 - c)
    up = (dom, lax.rem(z + 1, SZ) * 2 + c)
    down = (dom, lax.rem(z + SZ - 1, SZ) * 2 + c)

    def remote(src, dst, send, recv, device):
        return pltpu.make_async_remote_copy(
            src, dst, send, recv, device_id=device, device_id_type=MESH
        )

    def mate(step):
        return (dom, lax.rem(me + step, 2 * SZ))

    def x_mate(step):
        return (y * SX + lax.rem(x + step, SX), me)

    def y_mate(step):
        return (lax.rem(y + step, SY) * SX + x, me)

    def source(o):
        return lax.rem(x + SX - hop(o), SX)

    def strip(q, to):
        return pl.ds(pl.multiple_of(q * ROW + to * OUT, OUT), OUT)

    def local(q):
        return pl.ds(pl.multiple_of(q * OUT, OUT), OUT)

    barrier = pltpu.get_barrier_semaphore()

    def greet(device):
        pl.semaphore_signal(barrier, inc=1, device_id=device, device_id_type=MESH)

    greet(up)
    greet(down)
    for step in range(1, SX):
        greet(x_mate(step))
    greet(other)
    for q in range(SY):
        pltpu.make_async_copy(
            part_ref.at[:, strip(q, x)], gath.at[me, x, :, local(q)], local_sem
        ).start()
    for step in range(3, 2 * SZ - 2):
        greet(mate(step))
    greet(mate(2 * SZ - 1 - (2 * SZ - 2) * c))
    for step in range(1, SY):
        greet(y_mate(step))
    seen = pltpu.make_async_copy(focus_ref, few, focus_sem)
    seen.start()
    for q in range(SY):
        pltpu.make_async_copy(
            refs_ref.at[:, :, strip(q, x)], refs.at[:, :, local(q)], refs_sem
        ).start()
    for q in range(SY):
        pltpu.make_async_copy(
            noise_ref.at[:, strip(q, x)], noise.at[:, local(q)], noise_sem
        ).start()
    seen.wait()
    diagonal = lax.broadcasted_iota(jnp.int32, (8, 8), 0) == lax.broadcasted_iota(
        jnp.int32, (8, 8), 1
    )
    wide = jnp.broadcast_to(few[...].astype(F32), (8, 8))
    column = jnp.sum(jnp.where(diagonal, wide, 0.0), axis=1, keepdims=True)
    spread = twice(jnp.broadcast_to(column, (8, 128))).astype(BF16)
    focus[...] = spread
    gath[me, x, :, LOCAL:] = spread
    here = gath.at[me, x, :, pl.ds(0, LOCAL)]
    pltpu.make_async_copy(here, here, local_sem).wait()
    pl.semaphore_wait(barrier, 2 * SZ - 1 + SX - 1 + SY - 1)

    def ring_copy(way, step, o):
        block = lax.rem(z + SZ - step, SZ) if way == 0 else lax.rem(z + step, SZ)
        ref = gath.at[block * 2 + c, source(o)]
        return remote(
            ref, ref, ring_send.at[way, step, o], ring_recv.at[way, step, o],
            up if way == 0 else down,
        )

    def ring_landed(way, step, o):
        block = lax.rem(z + 2 * SZ - step - 1, SZ) if way == 0 else lax.rem(z + step + 1, SZ)
        ref = gath.at[block * 2 + c, source(o)]
        remote(
            ref, ref, ring_send.at[way, step, o], ring_recv.at[way, step, o],
            up if way == 0 else down,
        ).wait_recv()

    def core_copy(dist, o):
        ref = gath.at[lax.rem(z + dist, SZ) * 2 + c, source(o)]
        return remote(ref, ref, core_send.at[dist, o], core_recv.at[dist, o], other)

    def core_landed(dist, o):
        ref = gath.at[lax.rem(z + dist, SZ) * 2 + 1 - c, source(o)]
        remote(ref, ref, core_send.at[dist, o], core_recv.at[dist, o], other).wait_recv()

    def swap_landed(o):
        ref = gath.at[me, source(o)]
        remote(ref, ref, asend.at[o - 1], arecv.at[o - 1], x_mate(hop(o))).wait_recv()

    def term_copy(dist, o):
        ref = score.at[x, lax.rem(z + dist, SZ)]
        return remote(ref, ref, tsend.at[dist, o - 1], trecv.at[dist, o - 1], x_mate(hop(o)))

    def term_landed(dist, o):
        ref = score.at[source(o), lax.rem(z + dist, SZ)]
        remote(ref, ref, tsend.at[dist, o - 1], trecv.at[dist, o - 1], x_mate(hop(o))).wait_recv()

    def last_copy(u, o):
        at = pl.ds(pl.multiple_of(source(u) * 16, 16), 16)
        ref = score.at[x, lax.rem(z + HALFZ, SZ), at]
        return remote(ref, ref, lsend.at[u, o - 1], lrecv.at[u, o - 1], x_mate(hop(o)))

    def last_landed(u, o):
        row = lax.rem(source(o) + SX - hop(u), SX)
        at = pl.ds(pl.multiple_of(row * 16, 16), 16)
        ref = score.at[source(o), lax.rem(z + HALFZ, SZ), at]
        remote(ref, ref, lsend.at[u, o - 1], lrecv.at[u, o - 1], x_mate(hop(o))).wait_recv()

    def stat_copy(step):
        return remote(
            stat.at[me], stat.at[me], ssend.at[step - 1], srecv.at[step - 1], mate(step)
        )

    def stat_landed(step):
        ref = stat.at[lax.rem(me + 2 * SZ - step, 2 * SZ)]
        remote(ref, ref, ssend.at[step - 1], srecv.at[step - 1], mate(step)).wait_recv()

    ring_copy(0, 0, 0).start()
    ring_copy(1, 0, 0).start()
    for o in range(1, SX):
        to = lax.rem(x + hop(o), SX)
        for q in range(SY):
            remote(
                part_ref.at[:, strip(q, to)], gath.at[me, x, :, local(q)],
                asend.at[o - 1], arecv.at[o - 1], x_mate(hop(o)),
            ).start()
        remote(
            focus, gath.at[me, x, :, pl.ds(LOCAL, 128)],
            asend.at[o - 1], arecv.at[o - 1], x_mate(hop(o)),
        ).start()
    core_copy(0, 0).start()

    def tables_and_shifts(q, _):
        at = local(q)
        pixel = lax.broadcasted_iota(jnp.int32, (8, OUT), 1) + (q * ROW + x * OUT)
        fx = (lax.shift_right_logical(pixel, 6) - 64).astype(F32)
        fy = (pixel & 63).astype(F32)
        tab[0, :, at] = (fx * fx + fy * fy) * (INV_TWO_PI / 4096.0)
        tab[7, :, at] = jnp.broadcast_to(noise[:, at], (8, OUT))
        trig = []
        for turns in (fx * (1.0 / 64.0), fy * (1.0 / 64.0), (fx + fy) * (1.0 / 64.0)):
            trig.append((sin_turns(turns + 0.25), sin_turns(turns)))
        for t, (cos, sin) in enumerate(trig):
            tab[1 + 2 * t, :, at] = cos
            tab[2 + 2 * t, :, at] = sin
        for half in range(REFS // 16):
            rows = slice(16 * half, 16 * half + 16)
            real, imag = refs[0, rows, at], refs[1, rows, at]
            shf[0, rows, at] = real
            shf[1, rows, at] = imag
            real, imag = real.astype(F32), imag.astype(F32)
            power = (real * real + imag * imag).astype(BF16) * BF16(-0.5)
            for t in range(TRANS):
                to = slice(t * REFS + 16 * half, t * REFS + 16 * half + 16)
                shf[2, to, at] = power
                if t:
                    cos, sin = twice(trig[t - 1][0]), twice(trig[t - 1][1])
                    shf[0, to, at] = (real * cos - imag * sin).astype(BF16)
                    shf[1, to, at] = (real * sin + imag * cos).astype(BF16)
        for comp in range(3):
            turned[comp, at] = shf[comp, :, at].T
        return 0

    def first_hop(o, _):
        swap_landed(o)
        ring_copy(0, 0, o).start()
        ring_copy(1, 0, o).start()
        core_copy(0, o).start()
        return 0

    def weigh(dist, o):
        core_landed(dist, o)
        block, src = lax.rem(z + dist, SZ), source(o)
        rows = pl.ds(pl.multiple_of(block * 64 + src * 16, 16), 16)
        tail = pl.ds(LOCAL, 128)
        d0 = gath[2 * block, src, :, tail].astype(F32)[:8]
        d1 = gath[2 * block + 1, src, :, tail].astype(F32)[:8]
        d = jnp.concatenate([d0, d1], axis=0)
        d = jnp.concatenate([d] * (PART // 128), axis=1)

        def part(k, _):
            at = pl.ds(pl.multiple_of(k * PART, PART), PART)
            transfer = sin_turns(twice(tab[0, :, at]) * d + PHASE) * (-AMP)
            fac = transfer * twice(tab[7, :, at])
            wgt[2, rows, at] = (fac * transfer).astype(BF16)
            a = gath[2 * block, src, :, at].astype(F32)
            b = gath[2 * block + 1, src, :, at].astype(F32)
            for comp in range(2):
                pick = slice(8 * comp, 8 * comp + 8)
                both = jnp.concatenate([a[pick], b[pick]], axis=0)
                wgt[comp, rows, at] = (both * fac).astype(BF16)
            return 0

        lax.fori_loop(0, LOCAL // PART, part, 0)

    def dots(rows):
        acc = jnp.dot(wgt[0, rows], turned[0], preferred_element_type=F32)
        acc = acc + jnp.dot(wgt[1, rows], turned[1], preferred_element_type=F32)
        return acc + jnp.dot(wgt[2, rows], turned[2], preferred_element_type=F32)

    def terms(dist):
        block = lax.rem(z + dist, SZ)
        score[x, block] = dots(pl.ds(pl.multiple_of(block * 64, 64), 64))
        for o in range(1, SX):
            term_copy(dist, o).start()

    def last_terms(u):
        at, block = pl.ds(pl.multiple_of(source(u) * 16, 16), 16), lax.rem(z + HALFZ, SZ)
        score[x, block, at] = dots(pl.ds(pl.multiple_of(block * 64 + source(u) * 16, 16), 16))
        for o in range(1, SX):
            last_copy(u, o).start()

    def own(o, _):
        weigh(0, o)
        return 0

    def chunk_of(e):
        k, last = lax.rem(e, SX), e // (3 * SX)
        return k + last * (lax.rem(k, HALF) * HALF + k // HALF - k)

    def event(e, _):
        step, o = e // SX, chunk_of(e)
        for s in range(SZ // 2):

            @pl.when(step == s)
            def _():
                if s < 3:
                    for way in range(2):
                        ring_landed(way, s, o)
                    if s < 2:
                        for way in range(2):
                            ring_copy(way, s + 1, o).start()
                    else:

                        @pl.when(o < HALF)
                        def _():
                            ring_copy(0, 3, o).start()

                        @pl.when(o >= HALF)
                        def _():
                            ring_copy(1, 3, o).start()

                    core_copy(SZ - 1 - s, o).start()
                    core_copy(s + 1, o).start()
                else:

                    @pl.when(o < HALF)
                    def _():
                        ring_landed(0, 3, o)

                    @pl.when(o >= HALF)
                    def _():
                        ring_landed(1, 3, o)

                    core_copy(4, o).start()

        return 0

    def work(e):
        step, o = e // SX, chunk_of(e)
        ways = 2 - step // 3

        def chunk(way, _):
            weigh((1 - way) * (SZ - 1 - step) + way * (step + 1), o)
            return 0

        lax.fori_loop(0, ways, chunk, 0)

        @pl.when(step == 3)
        def _():
            last_terms(o)

        @pl.when((step < 3) & (o == SX - 1))
        def _():
            def block(way, _):
                terms((1 - way) * (SZ - 1 - step) + way * (step + 1))
                return 0

            lax.fori_loop(0, ways, block, 0)

    def turn(e, _):
        event(e, None)
        work(e - 1)
        return 0

    event(0, None)
    lax.fori_loop(1, SX, first_hop, 0)
    pltpu.make_async_copy(refs, refs, refs_sem).wait()
    pltpu.make_async_copy(noise, noise, noise_sem).wait()
    lax.fori_loop(0, SY, tables_and_shifts, 0)
    lax.fori_loop(0, SX, own, 0)
    terms(0)
    lax.fori_loop(1, 4 * SX, turn, 0)
    work(4 * SX - 1)

    for dist in range(SZ):
        if dist != HALFZ:
            for o in range(1, SX):
                term_landed(dist, o)
    for u in range(SX):
        for o in range(1, SX):
            last_landed(u, o)
    tops, totals = [], []
    for i in range(SZ // 2):
        rows = [
            (score[0, k] + score[1, k]) + (score[2, k] + score[3, k])
            for k in (2 * i, 2 * i + 1)
        ]
        block = jnp.concatenate(rows, axis=0).T
        top = jnp.max(block, axis=0, keepdims=True)
        tops.append(top)
        spread = jnp.exp(block - top)
        flip[:, i * 128 : (i + 1) * 128] = spread
        totals.append(jnp.sum(spread, axis=0, keepdims=True))
    stat[me] = jnp.concatenate(tops + totals, axis=0)
    for step in sorted(range(1, 2 * SZ), key=lambda k: abs(k - SZ)):
        stat_copy(step).start()
    for step in range(1, 2 * SZ):
        stat_landed(step)
    stats = stat[...]
    tops, totals = stats[:, 0:4], stats[:, 4:8]
    all_top = jnp.max(tops, axis=0)
    all_total = jnp.sum(totals * jnp.exp(tops - all_top[None]), axis=0)
    share = jnp.exp(stat[me, 0:4] - all_top) / all_total
    for i in range(SZ // 2):
        at = slice(i * 128, (i + 1) * 128)
        posterior = (flip[:, at] * share[i : i + 1]).astype(BF16)
        post[:, at] = posterior
        p = posterior.astype(F32)
        occ[:, at] = (
            p[0:REFS] + p[REFS : 2 * REFS] + p[2 * REFS : 3 * REFS] + p[3 * REFS :]
        ).astype(BF16)

    def y_step(i):
        j = (i + 1) // 2
        return 4 - j + 2 * j * lax.rem(i + 1, 2)

    top_half, low_half = slice(0, MID), slice(MID, 2 * MID)

    def y_copy(i, step, rows=slice(0, 2 * MID), sem=None):
        sem = i if sem is None else sem
        return remote(
            ysend.at[i, rows], yrecv.at[i, rows], ys_sem.at[sem], yr_sem.at[sem], y_mate(step)
        )

    def y_copies():
        return (
            y_copy(0, 2, top_half), y_copy(1, 1), y_copy(2, SY - 1), y_copy(3, 2),
            y_copy(4, SY - 2), y_copy(5, 1), y_copy(6, SY - 1), y_copy(0, SY - 2, low_half, 7),
        )

    def sums(i):
        at = local(lax.rem(y + y_step(i), SY))
        a0 = jnp.dot(post[...], wgt[0, :, at], preferred_element_type=F32)
        a1 = jnp.dot(post[...], wgt[1, :, at], preferred_element_type=F32)
        ctf = jnp.dot(occ[...], wgt[2, :, at], preferred_element_type=F32)
        real, imag = a0[0:REFS], a1[0:REFS]
        for t in range(1, TRANS):
            cos, sin = tab[2 * t - 1, :, at], tab[2 * t, :, at]
            cos = jnp.concatenate([cos] * (REFS // 8), axis=0)
            sin = jnp.concatenate([sin] * (REFS // 8), axis=0)
            b0, b1 = a0[t * REFS : (t + 1) * REFS], a1[t * REFS : (t + 1) * REFS]
            real = real + b0 * cos + b1 * sin
            imag = imag + b1 * cos - b0 * sin
        return real, imag, ctf

    def piece(i, _):
        real, imag, ctf = sums(i)

        @pl.when((i < 3) | (i == 5) | (i == 6))
        def _():
            ysend[i, 0:REFS] = real.astype(BF16)
            ysend[i, REFS : 2 * REFS] = imag.astype(BF16)
            ysend[i, 2 * REFS :] = ctf.astype(BF16)

        @pl.when((i == 3) | (i == 4))
        def _():
            hold[i - 3, 0:REFS] = real
            hold[i - 3, REFS : 2 * REFS] = imag
            hold[i - 3, 2 * REFS :] = ctf

        @pl.when(i == SY - 1)
        def _():
            total[0:REFS] = real
            total[REFS : 2 * REFS] = imag
            total[2 * REFS :] = ctf

        for k in (0, 1, 2, 5, 6):

            @pl.when(i == k)
            def _():
                y_copies()[k].start()
                if k == 0:
                    y_copies()[7].start()

        return 0

    lax.fori_loop(0, SY, piece, 0)

    near, far = y_copies()[1], y_copies()[0]
    near.wait_recv()
    far.wait_recv()
    both = hold[0] + yrecv[1].astype(F32)
    ysend[3, top_half] = (both[top_half] + yrecv[0, top_half].astype(F32)).astype(BF16)
    ysend[3, low_half] = both[low_half].astype(BF16)
    y_copies()[3].start()
    near, far = y_copies()[2], y_copies()[7]
    near.wait_recv()
    far.wait_recv()
    both = hold[1] + yrecv[2].astype(F32)
    ysend[4, top_half] = both[top_half].astype(BF16)
    ysend[4, low_half] = (both[low_half] + yrecv[0, low_half].astype(F32)).astype(BF16)
    y_copies()[4].start()

    y_copies()[5].wait_recv()
    y_copies()[6].wait_recv()
    total[...] += yrecv[5].astype(F32) + yrecv[6].astype(F32)
    y_copies()[3].wait_recv()
    y_copies()[4].wait_recv()
    total[...] += yrecv[3].astype(F32) + yrecv[4].astype(F32)
    weight = total[2 * REFS :] + REGULARIZER
    out_ref[0] = total[0:REFS] / weight
    out_ref[1] = total[REFS : 2 * REFS] / weight

    def drain_ring(o, _):
        for s in range(3):
            for way in range(2):
                ring_copy(way, s, o).wait_send()

        @pl.when(o < HALF)
        def _():
            ring_copy(0, 3, o).wait_send()

        @pl.when(o >= HALF)
        def _():
            ring_copy(1, 3, o).wait_send()

        return 0

    lax.fori_loop(0, SX, drain_ring, 0)

    def drain_blocks(dist, _):
        for o in range(SX):
            core_copy(dist, o).wait_send()

        @pl.when(dist != HALFZ)
        def _():
            for o in range(1, SX):
                term_copy(dist, o).wait_send()

        return 0

    lax.fori_loop(0, SZ, drain_blocks, 0)

    def drain_last(u, _):
        for o in range(1, SX):
            last_copy(u, o).wait_send()
        return 0

    lax.fori_loop(0, SX, drain_last, 0)

    def drain_swap(o, _):
        ref = gath.at[me, source(o)]
        remote(ref, ref, asend.at[o - 1], arecv.at[o - 1], x_mate(hop(o))).wait_send()
        return 0

    lax.fori_loop(1, SX, drain_swap, 0)

    def drain_stats(step, _):
        stat_copy(step).wait_send()
        return 0

    lax.fori_loop(1, 2 * SZ, drain_stats, 0)

    for copy in y_copies():
        copy.wait_send()


def shards(particles, defocus, references, noise_weights):
    dma = pltpu.SemaphoreType.DMA
    nblock = 2 * SZ
    rows = particles.shape[0] * particles.shape[1]
    vmem = pl.BlockSpec(memory_space=pltpu.VMEM)
    hbm = pl.BlockSpec(memory_space=pl.ANY)
    return pl.pallas_call(
        kernel,
        out_shape=pltpu.VMEM((2, REFS, OUT), F32),
        in_specs=[hbm, hbm, hbm, hbm],
        out_specs=vmem,
        scratch_shapes=[
            pltpu.VMEM((nblock, SX, rows, WIDE), BF16),
            pltpu.VMEM((rows, 128), BF16),
            pltpu.VMEM((1, 8), BF16),
            pltpu.VMEM((2, REFS, LOCAL), BF16),
            pltpu.VMEM((1, LOCAL), F32),
            pltpu.VMEM((8, 8, LOCAL), F32),
            pltpu.VMEM((3, NPART, LOCAL), BF16),
            pltpu.VMEM((3, NREF, LOCAL), BF16),
            pltpu.VMEM((3, LOCAL, NREF), BF16),
            pltpu.VMEM((SX, SZ, 64, NREF), F32),
            pltpu.VMEM((nblock, 8, 128), F32),
            pltpu.VMEM((NREF, NPART), F32),
            pltpu.VMEM((NREF, NPART), BF16),
            pltpu.VMEM((REFS, NPART), BF16),
            pltpu.VMEM((SY - 1, 3 * REFS, OUT), BF16),
            pltpu.VMEM((SY - 1, 3 * REFS, OUT), BF16),
            pltpu.VMEM((2, 3 * REFS, OUT), F32),
            pltpu.VMEM((3 * REFS, OUT), F32),
            dma,
            dma,
            dma,
            dma,
            dma((SX - 1,)),
            dma((SX - 1,)),
            dma((2, 4, SX)),
            dma((2, 4, SX)),
            dma((SZ, SX)),
            dma((SZ, SX)),
            dma((SZ, SX - 1)),
            dma((SZ, SX - 1)),
            dma((SX, SX - 1)),
            dma((SX, SX - 1)),
            dma((nblock - 1,)),
            dma((nblock - 1,)),
            dma((SY,)),
            dma((SY,)),
        ],
        name="expectation",
        compiler_params=pltpu.CompilerParams(
            collective_id=0, has_side_effects=True, vmem_limit_bytes=56 * 2**20
        ),
    )(
        particles.reshape(rows, PIX),
        defocus.reshape(1, 8),
        references,
        noise_weights.reshape(1, PIX),
    )


def solution(mesh):
    return jax.shard_map(
        shards,
        mesh=mesh,
        in_specs=(P(None, ("dom", "ref"), None), P(("dom", "ref")), P(None, "ref", None), P()),
        out_specs=P(None, "ref", "dom"),
        check_vma=False,
    )
```

```python
import jax
import jax.numpy as jnp
from jax import lax
from jax.experimental import pallas as pl
from jax.experimental.pallas import tpu as pltpu
from jax.sharding import PartitionSpec as P

PIX = 8192
TRANS = 4
REFS = 32
SX, SY, SZ = 4, 8, 8
OUT = 256
ROW = SX * OUT
LOCAL = SY * OUT
WIDE = LOCAL + 128
PART = 1024
HALF = SX // 2
HALFZ = SZ // 2
NREF = TRANS * REFS
MID = 3 * REFS // 2
NPART = SZ * SX * 16
REGULARIZER = 0.05

AMP = 1.000012499921876
PHASE = 0.015941940272471127
INV_TWO_PI = 0.15915494309189535
SIN_TERMS = (
    6.283182818554191,
    -41.341421398928475,
    81.5961838781331,
    -76.58010057017961,
    41.205395033387106,
    -12.271262585212861,
)

MESH = pl.DeviceIdType.MESH
F32 = jnp.float32
BF16 = jnp.bfloat16


def sin_turns(turns):
    v = turns - jnp.round(turns)
    sq = v * v
    acc = sq * SIN_TERMS[5] + SIN_TERMS[4]
    for term in SIN_TERMS[3::-1]:
        acc = acc * sq + term
    return acc * v


def hop(o):
    return o + (o // 2) * (5 - 2 * o)


def twice(a):
    return jnp.concatenate([a, a], axis=0)


def kernel(
    part_ref, focus_ref, refs_ref, noise_ref, out_ref,
    gath, focus, few, refs, noise, tab, wgt, shf, turned, score, stat, flip, post, occ, ysend, yrecv, hold, total,
    local_sem, refs_sem, noise_sem, focus_sem, asend, arecv, ring_send, ring_recv, core_send, core_recv,
    tsend, trecv, lsend, lrecv, ssend, srecv, ys_sem, yr_sem,
):
    dom, me = lax.axis_index("dom"), lax.axis_index("ref")
    y, x, z, c = dom // SX, dom % SX, me // 2, me % 2
    other = (dom, z * 2 + 1 - c)
    up = (dom, lax.rem(z + 1, SZ) * 2 + c)
    down = (dom, lax.rem(z + SZ - 1, SZ) * 2 + c)

    def remote(src, dst, send, recv, device):
        return pltpu.make_async_remote_copy(
            src, dst, send, recv, device_id=device, device_id_type=MESH
        )

    def mate(step):
        return (dom, lax.rem(me + step, 2 * SZ))

    def x_mate(step):
        return (y * SX + lax.rem(x + step, SX), me)

    def y_mate(step):
        return (lax.rem(y + step, SY) * SX + x, me)

    def source(o):
        return lax.rem(x + SX - hop(o), SX)

    def strip(q, to):
        return pl.ds(pl.multiple_of(q * ROW + to * OUT, OUT), OUT)

    def local(q):
        return pl.ds(pl.multiple_of(q * OUT, OUT), OUT)

    barrier = pltpu.get_barrier_semaphore()

    def greet(device):
        pl.semaphore_signal(barrier, inc=1, device_id=device, device_id_type=MESH)

    greet(up)
    greet(down)
    for step in range(1, SX):
        greet(x_mate(step))
    greet(other)
    for q in range(SY):
        pltpu.make_async_copy(
            part_ref.at[:, strip(q, x)], gath.at[me, x, :, local(q)], local_sem
        ).start()
    for step in range(3, 2 * SZ - 2):
        greet(mate(step))
    greet(mate(2 * SZ - 1 - (2 * SZ - 2) * c))
    for step in range(1, SY):
        greet(y_mate(step))
    seen = pltpu.make_async_copy(focus_ref, few, focus_sem)
    seen.start()
    for q in range(SY):
        pltpu.make_async_copy(
            refs_ref.at[:, :, strip(q, x)], refs.at[:, :, local(q)], refs_sem
        ).start()
    for q in range(SY):
        pltpu.make_async_copy(
            noise_ref.at[:, strip(q, x)], noise.at[:, local(q)], noise_sem
        ).start()
    seen.wait()
    diagonal = lax.broadcasted_iota(jnp.int32, (8, 8), 0) == lax.broadcasted_iota(
        jnp.int32, (8, 8), 1
    )
    wide = jnp.broadcast_to(few[...].astype(F32), (8, 8))
    column = jnp.sum(jnp.where(diagonal, wide, 0.0), axis=1, keepdims=True)
    spread = twice(jnp.broadcast_to(column, (8, 128))).astype(BF16)
    focus[...] = spread
    gath[me, x, :, LOCAL:] = spread
    here = gath.at[me, x, :, pl.ds(0, LOCAL)]
    pltpu.make_async_copy(here, here, local_sem).wait()
    pl.semaphore_wait(barrier, 2 * SZ - 1 + SX - 1 + SY - 1)

    def ring_copy(way, step, o):
        block = lax.rem(z + SZ - step, SZ) if way == 0 else lax.rem(z + step, SZ)
        ref = gath.at[block * 2 + c, source(o)]
        return remote(
            ref, ref, ring_send.at[way, step, o], ring_recv.at[way, step, o],
            up if way == 0 else down,
        )

    def ring_landed(way, step, o):
        block = lax.rem(z + 2 * SZ - step - 1, SZ) if way == 0 else lax.rem(z + step + 1, SZ)
        ref = gath.at[block * 2 + c, source(o)]
        remote(
            ref, ref, ring_send.at[way, step, o], ring_recv.at[way, step, o],
            up if way == 0 else down,
        ).wait_recv()

    def core_copy(dist, o):
        ref = gath.at[lax.rem(z + dist, SZ) * 2 + c, source(o)]
        return remote(ref, ref, core_send.at[dist, o], core_recv.at[dist, o], other)

    def core_landed(dist, o):
        ref = gath.at[lax.rem(z + dist, SZ) * 2 + 1 - c, source(o)]
        remote(ref, ref, core_send.at[dist, o], core_recv.at[dist, o], other).wait_recv()

    def swap_landed(o):
        ref = gath.at[me, source(o)]
        remote(ref, ref, asend.at[o - 1], arecv.at[o - 1], x_mate(hop(o))).wait_recv()

    def term_copy(dist, o):
        ref = score.at[x, lax.rem(z + dist, SZ)]
        return remote(ref, ref, tsend.at[dist, o - 1], trecv.at[dist, o - 1], x_mate(hop(o)))

    def term_landed(dist, o):
        ref = score.at[source(o), lax.rem(z + dist, SZ)]
        remote(ref, ref, tsend.at[dist, o - 1], trecv.at[dist, o - 1], x_mate(hop(o))).wait_recv()

    def last_copy(u, o):
        at = pl.ds(pl.multiple_of(source(u) * 16, 16), 16)
        ref = score.at[x, lax.rem(z + HALFZ, SZ), at]
        return remote(ref, ref, lsend.at[u, o - 1], lrecv.at[u, o - 1], x_mate(hop(o)))

    def last_landed(u, o):
        row = lax.rem(source(o) + SX - hop(u), SX)
        at = pl.ds(pl.multiple_of(row * 16, 16), 16)
        ref = score.at[source(o), lax.rem(z + HALFZ, SZ), at]
        remote(ref, ref, lsend.at[u, o - 1], lrecv.at[u, o - 1], x_mate(hop(o))).wait_recv()

    def stat_copy(step):
        return remote(
            stat.at[me], stat.at[me], ssend.at[step - 1], srecv.at[step - 1], mate(step)
        )

    def stat_landed(step):
        ref = stat.at[lax.rem(me + 2 * SZ - step, 2 * SZ)]
        remote(ref, ref, ssend.at[step - 1], srecv.at[step - 1], mate(step)).wait_recv()

    ring_copy(0, 0, 0).start()
    ring_copy(1, 0, 0).start()
    for o in range(1, SX):
        to = lax.rem(x + hop(o), SX)
        for q in range(SY):
            remote(
                part_ref.at[:, strip(q, to)], gath.at[me, x, :, local(q)],
                asend.at[o - 1], arecv.at[o - 1], x_mate(hop(o)),
            ).start()
        remote(
            focus, gath.at[me, x, :, pl.ds(LOCAL, 128)],
            asend.at[o - 1], arecv.at[o - 1], x_mate(hop(o)),
        ).start()
    core_copy(0, 0).start()

    def tables_and_shifts(q, _):
        at = local(q)
        pixel = lax.broadcasted_iota(jnp.int32, (8, OUT), 1) + (q * ROW + x * OUT)
        fx = (lax.shift_right_logical(pixel, 6) - 64).astype(F32)
        fy = (pixel & 63).astype(F32)
        tab[0, :, at] = (fx * fx + fy * fy) * (INV_TWO_PI / 4096.0)
        tab[7, :, at] = jnp.broadcast_to(noise[:, at], (8, OUT))
        trig = []
        for turns in (fx * (1.0 / 64.0), fy * (1.0 / 64.0), (fx + fy) * (1.0 / 64.0)):
            trig.append((sin_turns(turns + 0.25), sin_turns(turns)))
        for t, (cos, sin) in enumerate(trig):
            tab[1 + 2 * t, :, at] = cos
            tab[2 + 2 * t, :, at] = sin
        for half in range(REFS // 16):
            rows = slice(16 * half, 16 * half + 16)
            real, imag = refs[0, rows, at], refs[1, rows, at]
            shf[0, rows, at] = real
            shf[1, rows, at] = imag
            real, imag = real.astype(F32), imag.astype(F32)
            power = (real * real + imag * imag).astype(BF16) * BF16(-0.5)
            for t in range(TRANS):
                to = slice(t * REFS + 16 * half, t * REFS + 16 * half + 16)
                shf[2, to, at] = power
                if t:
                    cos, sin = twice(trig[t - 1][0]), twice(trig[t - 1][1])
                    shf[0, to, at] = (real * cos - imag * sin).astype(BF16)
                    shf[1, to, at] = (real * sin + imag * cos).astype(BF16)
        for comp in range(3):
            turned[comp, at] = shf[comp, :, at].T
        return 0

    def first_hop(o, _):
        swap_landed(o)
        ring_copy(0, 0, o).start()
        ring_copy(1, 0, o).start()
        core_copy(0, o).start()
        return 0

    def weigh(dist, o):
        core_landed(dist, o)
        block, src = lax.rem(z + dist, SZ), source(o)
        rows = pl.ds(pl.multiple_of(block * 64 + src * 16, 16), 16)
        tail = pl.ds(LOCAL, 128)
        d0 = gath[2 * block, src, :, tail].astype(F32)[:8]
        d1 = gath[2 * block + 1, src, :, tail].astype(F32)[:8]
        d = jnp.concatenate([d0, d1], axis=0)
        d = jnp.concatenate([d] * (PART // 128), axis=1)

        def part(k, _):
            at = pl.ds(pl.multiple_of(k * PART, PART), PART)
            transfer = sin_turns(twice(tab[0, :, at]) * d + PHASE) * (-AMP)
            fac = transfer * twice(tab[7, :, at])
            wgt[2, rows, at] = (fac * transfer).astype(BF16)
            a = gath[2 * block, src, :, at].astype(F32)
            b = gath[2 * block + 1, src, :, at].astype(F32)
            for comp in range(2):
                pick = slice(8 * comp, 8 * comp + 8)
                both = jnp.concatenate([a[pick], b[pick]], axis=0)
                wgt[comp, rows, at] = (both * fac).astype(BF16)
            return 0

        lax.fori_loop(0, LOCAL // PART, part, 0)

    def dots(rows):
        acc = jnp.dot(wgt[0, rows], turned[0], preferred_element_type=F32)
        acc = acc + jnp.dot(wgt[1, rows], turned[1], preferred_element_type=F32)
        return acc + jnp.dot(wgt[2, rows], turned[2], preferred_element_type=F32)

    def terms(dist):
        block = lax.rem(z + dist, SZ)
        score[x, block] = dots(pl.ds(pl.multiple_of(block * 64, 64), 64))
        for o in range(1, SX):
            term_copy(dist, o).start()

    def last_terms(u):
        at, block = pl.ds(pl.multiple_of(source(u) * 16, 16), 16), lax.rem(z + HALFZ, SZ)
        score[x, block, at] = dots(pl.ds(pl.multiple_of(block * 64 + source(u) * 16, 16), 16))
        for o in range(1, SX):
            last_copy(u, o).start()

    def own(o, _):
        weigh(0, o)
        return 0

    def chunk_of(e):
        k, last = lax.rem(e, SX), e // (3 * SX)
        return k + last * (lax.rem(k, HALF) * HALF + k // HALF - k)

    def event(e, _):
        step, o = e // SX, chunk_of(e)
        for s in range(SZ // 2):

            @pl.when(step == s)
            def _():
                if s < 3:
                    for way in range(2):
                        ring_landed(way, s, o)
                        if s < 2:
                            ring_copy(way, s + 1, o).start()
                    if s == 2:

                        @pl.when(o < HALF)
                        def _():
                            ring_copy(0, 3, o).start()

                        @pl.when(o >= HALF)
                        def _():
                            ring_copy(1, 3, o).start()

                    core_copy(SZ - 1 - s, o).start()
                    core_copy(s + 1, o).start()
                else:

                    @pl.when(o < HALF)
                    def _():
                        ring_landed(0, 3, o)

                    @pl.when(o >= HALF)
                    def _():
                        ring_landed(1, 3, o)

                    core_copy(4, o).start()

        return 0

    def work(e):
        step, o = e // SX, chunk_of(e)
        ways = 2 - step // 3

        def chunk(way, _):
            weigh((1 - way) * (SZ - 1 - step) + way * (step + 1), o)
            return 0

        lax.fori_loop(0, ways, chunk, 0)

        @pl.when(step == 3)
        def _():
            last_terms(o)

        @pl.when((step < 3) & (o == SX - 1))
        def _():
            def block(way, _):
                terms((1 - way) * (SZ - 1 - step) + way * (step + 1))
                return 0

            lax.fori_loop(0, ways, block, 0)

    def turn(e, _):
        event(e, None)
        work(e - 1)
        return 0

    event(0, None)
    lax.fori_loop(1, SX, first_hop, 0)
    pltpu.make_async_copy(refs, refs, refs_sem).wait()
    pltpu.make_async_copy(noise, noise, noise_sem).wait()
    lax.fori_loop(0, SY, tables_and_shifts, 0)
    lax.fori_loop(0, SX, own, 0)
    terms(0)
    lax.fori_loop(1, 4 * SX, turn, 0)
    work(4 * SX - 1)

    for dist in range(SZ):
        if dist != HALFZ:
            for o in range(1, SX):
                term_landed(dist, o)
    for u in range(SX):
        for o in range(1, SX):
            last_landed(u, o)
    tops, totals = [], []
    for i in range(SZ // 2):
        rows = [
            (score[0, k] + score[1, k]) + (score[2, k] + score[3, k])
            for k in (2 * i, 2 * i + 1)
        ]
        block = jnp.concatenate(rows, axis=0).T
        top = jnp.max(block, axis=0, keepdims=True)
        tops.append(top)
        spread = jnp.exp(block - top)
        flip[:, i * 128 : (i + 1) * 128] = spread
        totals.append(jnp.sum(spread, axis=0, keepdims=True))
    stat[me] = jnp.concatenate(tops + totals, axis=0)
    for step in sorted(range(1, 2 * SZ), key=lambda k: abs(k - SZ)):
        stat_copy(step).start()
    for step in range(1, 2 * SZ):
        stat_landed(step)
    stats = stat[...]
    tops, totals = stats[:, 0:4], stats[:, 4:8]
    all_top = jnp.max(tops, axis=0)
    all_total = jnp.sum(totals * jnp.exp(tops - all_top[None]), axis=0)
    share = jnp.exp(stat[me, 0:4] - all_top) / all_total
    for i in range(SZ // 2):
        at = slice(i * 128, (i + 1) * 128)
        posterior = (flip[:, at] * share[i : i + 1]).astype(BF16)
        post[:, at] = posterior
        p = posterior.astype(F32)
        occ[:, at] = (
            p[0:REFS] + p[REFS : 2 * REFS] + p[2 * REFS : 3 * REFS] + p[3 * REFS :]
        ).astype(BF16)

    def y_step(i):
        j = (i + 1) // 2
        return 4 - j + 2 * j * lax.rem(i + 1, 2)

    top_half, low_half = slice(0, MID), slice(MID, 2 * MID)

    def y_copy(i, step, rows=slice(0, 2 * MID), sem=None):
        sem = i if sem is None else sem
        return remote(
            ysend.at[i, rows], yrecv.at[i, rows], ys_sem.at[sem], yr_sem.at[sem], y_mate(step)
        )

    def y_copies():
        return (
            y_copy(0, 2, top_half), y_copy(1, 1), y_copy(2, SY - 1), y_copy(3, 2),
            y_copy(4, SY - 2), y_copy(5, 1), y_copy(6, SY - 1), y_copy(0, SY - 2, low_half, 7),
        )

    def sums(i):
        at = local(lax.rem(y + y_step(i), SY))
        a0 = jnp.dot(post[...], wgt[0, :, at], preferred_element_type=F32)
        a1 = jnp.dot(post[...], wgt[1, :, at], preferred_element_type=F32)
        ctf = jnp.dot(occ[...], wgt[2, :, at], preferred_element_type=F32)
        real, imag = a0[0:REFS], a1[0:REFS]
        for t in range(1, TRANS):
            cos, sin = tab[2 * t - 1, :, at], tab[2 * t, :, at]
            cos = jnp.concatenate([cos] * (REFS // 8), axis=0)
            sin = jnp.concatenate([sin] * (REFS // 8), axis=0)
            b0, b1 = a0[t * REFS : (t + 1) * REFS], a1[t * REFS : (t + 1) * REFS]
            real = real + b0 * cos + b1 * sin
            imag = imag + b1 * cos - b0 * sin
        return real, imag, ctf

    def piece(i, _):
        real, imag, ctf = sums(i)

        @pl.when((i < 3) | (i == 5) | (i == 6))
        def _():
            ysend[i, 0:REFS] = real.astype(BF16)
            ysend[i, REFS : 2 * REFS] = imag.astype(BF16)
            ysend[i, 2 * REFS :] = ctf.astype(BF16)

        @pl.when((i == 3) | (i == 4))
        def _():
            hold[i - 3, 0:REFS] = real
            hold[i - 3, REFS : 2 * REFS] = imag
            hold[i - 3, 2 * REFS :] = ctf

        @pl.when(i == SY - 1)
        def _():
            total[0:REFS] = real
            total[REFS : 2 * REFS] = imag
            total[2 * REFS :] = ctf

        for k in (0, 1, 2, 5, 6):

            @pl.when(i == k)
            def _():
                y_copies()[k].start()
                if k == 0:
                    y_copies()[7].start()

        return 0

    lax.fori_loop(0, SY, piece, 0)

    near, far = y_copies()[1], y_copies()[0]
    near.wait_recv()
    far.wait_recv()
    both = hold[0] + yrecv[1].astype(F32)
    ysend[3, top_half] = (both[top_half] + yrecv[0, top_half].astype(F32)).astype(BF16)
    ysend[3, low_half] = both[low_half].astype(BF16)
    y_copies()[3].start()
    near, far = y_copies()[2], y_copies()[7]
    near.wait_recv()
    far.wait_recv()
    both = hold[1] + yrecv[2].astype(F32)
    ysend[4, top_half] = both[top_half].astype(BF16)
    ysend[4, low_half] = (both[low_half] + yrecv[0, low_half].astype(F32)).astype(BF16)
    y_copies()[4].start()

    y_copies()[5].wait_recv()
    y_copies()[6].wait_recv()
    total[...] += yrecv[5].astype(F32) + yrecv[6].astype(F32)
    y_copies()[3].wait_recv()
    y_copies()[4].wait_recv()
    total[...] += yrecv[3].astype(F32) + yrecv[4].astype(F32)
    weight = total[2 * REFS :] + REGULARIZER
    out_ref[0] = total[0:REFS] / weight
    out_ref[1] = total[REFS : 2 * REFS] / weight

    def drain_ring(o, _):
        for s in range(3):
            for way in range(2):
                ring_copy(way, s, o).wait_send()

        @pl.when(o < HALF)
        def _():
            ring_copy(0, 3, o).wait_send()

        @pl.when(o >= HALF)
        def _():
            ring_copy(1, 3, o).wait_send()

        return 0

    lax.fori_loop(0, SX, drain_ring, 0)

    def drain_blocks(dist, _):
        for o in range(SX):
            core_copy(dist, o).wait_send()

        @pl.when(dist != HALFZ)
        def _():
            for o in range(1, SX):
                term_copy(dist, o).wait_send()

        return 0

    lax.fori_loop(0, SZ, drain_blocks, 0)

    def drain_last(u, _):
        for o in range(1, SX):
            last_copy(u, o).wait_send()
        return 0

    lax.fori_loop(0, SX, drain_last, 0)

    def drain_swap(o, _):
        ref = gath.at[me, source(o)]
        remote(ref, ref, asend.at[o - 1], arecv.at[o - 1], x_mate(hop(o))).wait_send()
        return 0

    lax.fori_loop(1, SX, drain_swap, 0)

    def drain_stats(step, _):
        stat_copy(step).wait_send()
        return 0

    lax.fori_loop(1, 2 * SZ, drain_stats, 0)

    for copy in y_copies():
        copy.wait_send()


def shards(particles, defocus, references, noise_weights):
    dma = pltpu.SemaphoreType.DMA
    nblock = 2 * SZ
    rows = particles.shape[0] * particles.shape[1]
    vmem = pl.BlockSpec(memory_space=pltpu.VMEM)
    hbm = pl.BlockSpec(memory_space=pl.ANY)
    return pl.pallas_call(
        kernel,
        out_shape=pltpu.VMEM((2, REFS, OUT), F32),
        in_specs=[hbm, hbm, hbm, hbm],
        out_specs=vmem,
        scratch_shapes=[
            pltpu.VMEM((nblock, SX, rows, WIDE), BF16),
            pltpu.VMEM((rows, 128), BF16),
            pltpu.VMEM((1, 8), BF16),
            pltpu.VMEM((2, REFS, LOCAL), BF16),
            pltpu.VMEM((1, LOCAL), F32),
            pltpu.VMEM((8, 8, LOCAL), F32),
            pltpu.VMEM((3, NPART, LOCAL), BF16),
            pltpu.VMEM((3, NREF, LOCAL), BF16),
            pltpu.VMEM((3, LOCAL, NREF), BF16),
            pltpu.VMEM((SX, SZ, 64, NREF), F32),
            pltpu.VMEM((nblock, 8, 128), F32),
            pltpu.VMEM((NREF, NPART), F32),
            pltpu.VMEM((NREF, NPART), BF16),
            pltpu.VMEM((REFS, NPART), BF16),
            pltpu.VMEM((SY - 1, 3 * REFS, OUT), BF16),
            pltpu.VMEM((SY - 1, 3 * REFS, OUT), BF16),
            pltpu.VMEM((2, 3 * REFS, OUT), F32),
            pltpu.VMEM((3 * REFS, OUT), F32),
            dma,
            dma,
            dma,
            dma,
            dma((SX - 1,)),
            dma((SX - 1,)),
            dma((2, 4, SX)),
            dma((2, 4, SX)),
            dma((SZ, SX)),
            dma((SZ, SX)),
            dma((SZ, SX - 1)),
            dma((SZ, SX - 1)),
            dma((SX, SX - 1)),
            dma((SX, SX - 1)),
            dma((nblock - 1,)),
            dma((nblock - 1,)),
            dma((SY,)),
            dma((SY,)),
        ],
        name="expectation",
        compiler_params=pltpu.CompilerParams(
            collective_id=0, has_side_effects=True, vmem_limit_bytes=56 * 2**20
        ),
    )(
        particles.reshape(rows, PIX),
        defocus.reshape(1, 8),
        references,
        noise_weights.reshape(1, PIX),
    )


def solution(mesh):
    return jax.shard_map(
        shards,
        mesh=mesh,
        in_specs=(P(None, ("dom", "ref"), None), P(("dom", "ref")), P(None, "ref", None), P()),
        out_specs=P(None, "ref", "dom"),
        check_vma=False,
    )
```
